512 devices in a mesh: blk: 128 (over z, y, core), col: 4 (over x).
Axes of the slice: x: 4, y: 4, z: 16, core: 2. Of those that a mesh axis runs over, the one named last changes fastest.
Arguments:
- panel: float32 [1, 32768, 512], P(None, 'blk')
- trailing: float32 [1, 32768, 2048], P(None, 'blk', 'col'), may hold values from -6 to 6
- pattern: int32 [2, 128], replicated, may hold values from 0 to 1, as said below
- target_rows: int32 [8], P('col'), may hold values from 2 to 127, as said below
Outputs:
- factor: float32 [1, 32768, 512], P(None, 'blk')
- schur_out: float32 [1, 32768, 2048], P(None, 'blk', 'col')
The draws below stay inside these ranges and needn't reach their ends.
Inputs may be any that keep to these rules, and one draw needn't show every extreme that they name: `pattern`: entries of block rows 0 and 1 are 1; entry (0, 127) is 0. `target_rows`: 8 distinct block rows, among them 2 and 127.
All inputs are finite; a program needn't handle non-finite values.
Results may differ from the reference program's by a relative error of at most 0.00007.
Values sent between devices are 32-bit elements; how exact they have to be, the bound alone decides.
No kernel may reach another device: no remote copies, remote signals or barrier semaphores. Data moves between devices by JAX's collectives and lax.ppermute only.
A program may use at most 64 MiB of HBM per device.

```python
import jax
import jax.numpy as jnp
from jax import lax

B = 256
BR_DEV = 1
NBR = 128
NTC = 8
ROWS = 32768
COLS = 2048


def draw_panel(key, part):
    key = jax.random.fold_in(key, 3)
    first_key, second_key, third_key = jax.random.split(key, 3)
    base_draw = 0.4 * jax.random.normal(first_key, (BR_DEV, ROWS, 2 * B), jnp.float32)
    width = 2 * B
    reach = 2.5 / (width - 1)
    raw_draw = jax.random.uniform(second_key, (width, width), jnp.float32, 0.0, 1.0)
    positions = jnp.arange(width)
    lift = jax.random.uniform(third_key, (width,), jnp.float32, 0.02, 0.4)
    coupling = reach * 0.5 * (raw_draw + raw_draw.T)
    identity = (positions[:, None] == positions[None, :]).astype(jnp.float32)
    diagonal = reach * (width - 1) * (1.0 + lift)
    pivot_block = identity * diagonal[None, :] - coupling * (1.0 - identity)
    return base_draw.at[0, :2 * B, :].set(pivot_block)


def draw_pattern(key, part):
    first_key, second_key = jax.random.split(key, 2)
    density = jax.random.randint(first_key, (1, NBR), 200, 950)
    draw_bits = jax.random.randint(second_key, (2, NBR), 0, 1000)
    pattern = (draw_bits < density).astype(jnp.int32)
    pattern = pattern.at[:, :2].set(1)
    return pattern.at[0, NBR - 1].set(0)


def draw_target_rows(key, part):
    first_key, second_key = jax.random.split(jax.random.fold_in(key, 7), 2)
    middle = jax.random.permutation(first_key, jnp.arange(3, NBR - 1, dtype=jnp.int32))[:NTC - 2]
    pinned = jnp.concatenate([jnp.array([2, NBR - 1], dtype=jnp.int32), middle])
    return jax.random.permutation(second_key, pinned)


def shard_levels(stream_key, extent, shards, low, high):
    def one(axis_at, parts):
        heights = jax.random.uniform(jax.random.fold_in(jax.random.fold_in(stream_key, 6), axis_at), (parts,), jnp.float32, low / len(shards), high / len(shards))
        return jnp.repeat(jnp.exp(heights), extent[axis_at] // parts).reshape((-1,) + (1,) * (len(extent) - axis_at - 1))

    level = one(*shards[0])
    for cut in shards[1:]:
        level = level * one(*cut)
    return level


def centred(rng, shape, spread, bound, cuts=(), kind=jnp.bfloat16):
    result = spread * jax.random.normal(rng, shape, jnp.float32)
    if cuts:
        result = result * shard_levels(rng, shape, cuts, -0.22, 0.18)
    return jnp.clip(result, -bound, bound).astype(kind)


def setup_inputs(seed: int = 0) -> dict:
    arg_keys = jax.random.split(jax.random.key(seed), 5)
    panel = draw_panel(jax.random.fold_in(arg_keys[4], 71), 0)
    trailing = centred(arg_keys[1], (BR_DEV, ROWS, COLS), 1.0, 6.0, ((1, 128), (2, 4)), jnp.float32)
    pattern = draw_pattern(jax.random.fold_in(arg_keys[4], 71), 0)
    target_rows = draw_target_rows(jax.random.fold_in(arg_keys[4], 71), 0)
    return {"panel": panel, "trailing": trailing, "pattern": pattern, "target_rows": target_rows}


def right_solve(factor_block, values):
    return lax.linalg.triangular_solve(factor_block, values, left_side=False, lower=True, transpose_a=True)

def reference(panel, trailing, pattern, target_rows):
    highest = lax.Precision.HIGHEST
    front_rows = panel.reshape(NBR, B, 2 * B)
    first_mask = pattern[0].astype(jnp.float32)
    second_mask = pattern[1].astype(jnp.float32)
    pivot_lead = jnp.linalg.cholesky(front_rows[0, :, :B])
    lower_left = right_solve(pivot_lead, front_rows[1, :, :B])
    inner_block = front_rows[1, :, B:] - jnp.dot(lower_left, lower_left.T, precision=highest)
    pivot_next = jnp.linalg.cholesky(inner_block)
    first_part = (front_rows[:, :, :B] * first_mask[:, None, None]).reshape(NBR * B, B)
    panel_one = right_solve(pivot_lead, first_part)
    second_part = (front_rows[:, :, B:] * second_mask[:, None, None]).reshape(NBR * B, B)
    second_part = second_part - jnp.dot(panel_one, lower_left.T, precision=highest)
    panel_two = right_solve(pivot_next, second_part)
    factor = jnp.concatenate([panel_one, panel_two], axis=1).reshape(NBR, B, 2 * B)
    top_row = jnp.concatenate([pivot_lead, jnp.zeros_like(pivot_lead)], axis=1)
    next_row = jnp.concatenate([lower_left, pivot_next], axis=1)
    factor = factor.at[0].set(top_row).at[1].set(next_row)
    columns = factor[target_rows.astype(jnp.int32)].reshape(NTC * B, 2 * B)
    flat_factor = factor.reshape(NBR * B, 2 * B)
    update = jnp.dot(flat_factor, columns.T, precision=highest)
    keep_rows = jnp.repeat((jnp.arange(NBR) >= 2).astype(jnp.float32), B)[:, None]
    schur_out = trailing.reshape(NBR * B, NTC * B) - keep_rows * update
    return (factor.reshape(BR_DEV, ROWS, 2 * B), schur_out.reshape(BR_DEV, ROWS, NTC * B))
```

```python
import jax
import jax.numpy as jnp
from jax import lax
from jax.sharding import Mesh, PartitionSpec as P

Z, Y2 = 16, 8


def right_solve(factor_block, values):
    return lax.linalg.triangular_solve(
        factor_block, values, left_side=False, lower=True, transpose_a=True
    )


def hdot(a, b):
    return jnp.dot(a, b, precision=lax.Precision.HIGHEST)


def local(panel, trailing, pattern, target_rows):
    _, size, width = panel.shape
    half = width // 2
    nz, npl, nx = lax.axis_size("z"), lax.axis_size("p"), lax.axis_size("x")
    iz, ip, ix = lax.axis_index("z"), lax.axis_index("p"), lax.axis_index("x")
    row = iz * npl + ip
    count = target_rows.shape[0]
    own = panel[0]
    fine = size // (npl * nx)
    coarse = size // npl
    by_piece = own.reshape(npl, nx, fine, width)
    mine = lax.dynamic_index_in_dim(by_piece, ix, 1, keepdims=False)
    got = lax.all_to_all(mine, "p", 0, 0)
    piece = jnp.concatenate([got[0, :, :half], got[1, :, :half], got[1, :, half:]], axis=0)
    along = lax.all_to_all(jnp.broadcast_to(piece[None], (nz,) + piece.shape), "z", 0, 0)
    piece = along[0]
    full = lax.all_to_all(
        jnp.broadcast_to(piece[None], (npl * nx,) + piece.shape), ("p", "x"), 0, 0
    )
    a00 = full[:, :fine].reshape(size, half)
    a10 = full[:, fine : 2 * fine].reshape(size, half)
    a11 = full[:, 2 * fine :].reshape(size, half)
    pieces = lax.all_to_all(own.reshape(npl, coarse, width), "p", 0, 0)
    sub = coarse // nz
    chosen = jnp.stack(
        [lax.dynamic_index_in_dim(pieces, target_rows[t] % npl, 0, False) for t in range(count)]
    )
    chosen = chosen.reshape(count, nz, sub, width).transpose(1, 0, 2, 3)
    chosen = chosen.reshape(nz, count * sub * width // 128, 128)
    got = lax.all_to_all(chosen, "z", 0, 0)
    got = got.reshape(nz, count, sub * width // 128, 128)
    held = jnp.stack(
        [
            lax.dynamic_index_in_dim(got[:, t], target_rows[t] // npl, 0, False)
            for t in range(count)
        ]
    ).reshape(count * sub * width // 128, 128)
    held = lax.all_to_all(jnp.broadcast_to(held[None], (nz,) + held.shape), "z", 0, 0)
    held = held.reshape(nz, count, sub, width).transpose(1, 0, 2, 3).reshape(count, coarse, width)
    held = lax.all_to_all(jnp.broadcast_to(held[None], (npl,) + held.shape), "p", 0, 0)
    targets = held.transpose(1, 0, 2, 3).reshape(count, size, width)
    l00 = jnp.linalg.cholesky(a00)
    l10 = right_solve(l00, a10)
    l11 = jnp.linalg.cholesky(a11 - hdot(l10, l10.T))
    which = jnp.concatenate([row[None], target_rows])
    hot = (jnp.arange(pattern.shape[1])[None, :] == which[:, None]).astype(jnp.int32)
    flags = jnp.sum(hot[None] * pattern[:, None, :], axis=2).astype(jnp.float32)
    rows = jnp.concatenate([own[None], targets])
    first = (rows[:, :, :half] * flags[0][:, None, None]).reshape(-1, half)
    second = (rows[:, :, half:] * flags[1][:, None, None]).reshape(-1, half)
    one = right_solve(l00, first)
    two = right_solve(l11, second - hdot(one, l10.T))
    solved = jnp.concatenate([one, two], axis=1)
    top = jnp.concatenate([l00, jnp.zeros_like(l00)], axis=1)
    nxt = jnp.concatenate([l10, l11], axis=1)
    mine = jnp.where(row == 0, top, jnp.where(row == 1, nxt, solved[:size]))
    update = lax.dot_general(
        mine, solved[size:], (((1,), (1,)), ((), ())), precision=lax.Precision.HIGHEST
    )
    schur = trailing[0] - jnp.where(row >= 2, update, 0.0)
    return mine[None], schur[None]


def solution(mesh):
    blk, col = mesh.devices.shape
    inner = Mesh(mesh.devices.reshape(blk // Y2, Y2, col), ("z", "p", "x"))
    rows = ("z", "p")
    in_specs = (P(None, rows, None), P(None, rows, "x"), P(), P("x"))
    out_specs = (P(None, rows, None), P(None, rows, "x"))
    return jax.shard_map(local, mesh=inner, in_specs=in_specs, out_specs=out_specs, check_vma=False)
```

```python
import jax
import jax.numpy as jnp
from jax import lax
from jax.experimental import pallas as pl
from jax.experimental.pallas import tpu as pltpu
from jax.sharding import Mesh, PartitionSpec as P

PLANE = 8
PANEL = 32
HIGHEST = lax.Precision.HIGHEST
OUTER = (((0,), (0,)), ((), ()))
ROWS = (((1,), (1,)), ((), ()))


def split(x):
    high = x.astype(jnp.bfloat16)
    rest = x - high.astype(jnp.float32)
    mid = rest.astype(jnp.bfloat16)
    low = (rest - mid.astype(jnp.float32)).astype(jnp.bfloat16)
    return high, mid, low


def outer(left, right):
    a, b, c = split(left)
    h, m, l = split(right)
    return lax.dot_general(
        jnp.concatenate([a, a, b, a, b, c], axis=0),
        jnp.concatenate([h, m, h, l, m, h], axis=0),
        OUTER,
        preferred_element_type=jnp.float32,
    )


def recip(d):
    r = pl.reciprocal(d, approx=True)
    return r * (2.0 - d * r)


def lane_block(x, lo, count):
    lane = lax.broadcasted_iota(jnp.int32, x.shape, 1)
    return (lane >= lo) & (lane < lo + count)


def inverse_factor(matrix):
    n = matrix.shape[0]
    groups, tiles = PANEL // 8, n // 128
    sub = lax.broadcasted_iota(jnp.int32, (8, 128), 0)
    lane = lax.broadcasted_iota(jnp.int32, (8, 128), 1)
    rest = matrix
    done = []
    for j in range(n // PANEL):
        lo = PANEL * j
        rows, rest = rest[:PANEL], rest[PANEL:]
        tile, off = lo // 128, lo % 128
        cols = [
            [
                jnp.broadcast_to(rows[8 * g : 8 * g + 8, lo + k : lo + k + 1], (8, 128))
                if g >= k // 8
                else None
                for g in range(groups)
            ]
            for k in range(PANEL)
        ]
        u = [
            [rows[8 * g : 8 * g + 8, 128 * c : 128 * c + 128] for c in range(tiles)]
            for g in range(groups)
        ]
        for g in range(groups):
            eye = (lane - off == sub + 8 * g).astype(jnp.float32)
            u[g][tile] = jnp.where(lane_block(eye, off, PANEL), eye, u[g][tile])
        scale = [jnp.zeros((8, 128), jnp.float32)] * groups
        for k in range(PANEL):
            at, s = k // 8, k % 8
            col = cols[k]
            d = jnp.broadcast_to(col[at][s : s + 1], (8, 128))
            r = recip(d)
            scale[at] = jnp.where(sub == s, lax.rsqrt(d), scale[at])
            if k == PANEL - 1:
                break
            low = [None] * at + [jnp.where(sub > s, col[at], 0.0)] + col[at + 1 :]
            ratio = [None if x is None else x * r for x in low]
            for i in range(k + 1, PANEL):
                first = i // 8
                b = jnp.broadcast_to(col[first][i % 8 : i % 8 + 1], (8, 128))
                for g in range(first, groups):
                    if i == k + 1:
                        cols[i][g] = cols[i][g] - (low[g] * b) * r
                    else:
                        cols[i][g] = cols[i][g] - ratio[g] * b
            for c in range(tiles):
                b = jnp.broadcast_to(u[at][c][s : s + 1], (8, 128))
                for g in range(at if s < 7 else at + 1, groups):
                    u[g][c] = u[g][c] - ratio[g] * b
        u = jnp.concatenate(
            [
                jnp.concatenate([x * scale[g] for x in u[g]], axis=1)
                for g in range(groups)
            ],
            axis=0,
        )
        done.append(u)
        left = rest.shape[0]
        if left:
            update = outer(u[:, 128 * ((lo + PANEL) // 128) :], u)
            update = update[update.shape[0] - left :]
            rest = jnp.where(lane_block(rest, lo, PANEL), 0.0, rest) - update
    full = jnp.concatenate(done, axis=0)
    row = lax.broadcasted_iota(jnp.int32, full.shape, 0)
    column = lax.broadcasted_iota(jnp.int32, full.shape, 1)
    return jnp.where(row >= column, full, 0.0)


def pivot_kernel(a00, a10, a11, lead, below, second):
    inv = inverse_factor(a00[...])
    lead[...] = inv
    l10 = lax.dot_general(
        a10[...], inv, ROWS, precision=HIGHEST, preferred_element_type=jnp.float32
    )
    below[...] = l10
    inner = a11[...] - lax.dot_general(
        l10, l10, ROWS, precision=HIGHEST, preferred_element_type=jnp.float32
    )
    second[...] = inverse_factor(inner)


def pivots(a00, a10, a11):
    like = jax.ShapeDtypeStruct(a00.shape, jnp.float32)
    return pl.pallas_call(
        pivot_kernel,
        out_shape=(like, like, like),
        compiler_params=pltpu.CompilerParams(vmem_limit_bytes=24 << 20),
        cost_estimate=pl.CostEstimate(
            flops=1 << 30, bytes_accessed=6 << 18, transcendentals=0
        ),
    )(a00, a10, a11)


def times_t(a, b):
    return lax.dot_general(a, b, ROWS, precision=lax.Precision.HIGHEST)


def copies(x, count):
    return jnp.broadcast_to(x[None], (count,) + x.shape)


def pick(x, at, axis):
    return lax.dynamic_index_in_dim(x, at, axis, keepdims=False)


def local(panel, trailing, pattern, target_rows):
    _, size, width = panel.shape
    half = width // 2
    nz, npl, nx = lax.axis_size("z"), lax.axis_size("p"), lax.axis_size("x")
    iz, ip, ix = lax.axis_index("z"), lax.axis_index("p"), lax.axis_index("x")
    row = iz * npl + ip
    count = target_rows.shape[0]
    own = panel[0]
    fine, coarse = size // (npl * nx), size // npl
    sub = coarse // nz
    pieces = lax.all_to_all(own.reshape(npl, coarse, width), "p", 0, 0)
    share = lax.dynamic_slice_in_dim(pieces[:2], ix * fine, fine, 1)
    share = jnp.concatenate(
        [share[0, :, :half], share[1, :, :half], share[1, :, half:]], axis=0
    )
    share = jnp.concatenate([share[:, :128], share[:, 128:]], axis=0)
    chosen = jnp.stack([pick(pieces, target_rows[t] % npl, 0) for t in range(count)])
    chosen = chosen.reshape(count, nz, sub, width).transpose(1, 0, 2, 3)
    chosen = chosen.reshape(nz, count * sub * width // 128, 128)
    along = lax.all_to_all(jnp.concatenate([copies(share, nz), chosen], axis=1), "z", 0, 0)
    depth = share.shape[0]
    full = lax.all_to_all(copies(along[0, :depth], npl * nx), ("p", "x"), 0, 0)
    full = full.reshape(npl * nx, 2, 3, fine, 128).transpose(2, 0, 3, 1, 4)
    full = full.reshape(3, size, half)
    lead, l10, second = pivots(full[0], full[1], full[2])
    got = along[:, depth:].reshape(nz, count, sub * width // 128, 128)
    held = jnp.concatenate([pick(got[:, t], target_rows[t] // npl, 0) for t in range(count)])
    held = lax.all_to_all(copies(held, nz), "z", 0, 0)
    held = held.reshape(nz, count, sub, width).transpose(1, 0, 2, 3).reshape(count, coarse, width)
    held = lax.all_to_all(copies(held, npl), "p", 0, 0)
    targets = held.transpose(1, 0, 2, 3).reshape(count * size, width)
    which = jnp.concatenate([row[None], target_rows])
    hot = (jnp.arange(pattern.shape[1])[None, :] == which[:, None]).astype(jnp.int32)
    flags = jnp.sum(hot[None] * pattern[:, None, :], axis=2).astype(jnp.float32)

    def solve(block, flag):
        one = times_t(block[:, :half] * flag[0], lead)
        two = times_t(block[:, half:] * flag[1] - times_t(one, l10), second)
        return one, two

    one, two = solve(own, flags[:, 0])
    lower = jnp.tril(jnp.ones((size, half), jnp.bool_))
    one = jnp.where((row == 0) & ~lower, 0.0, one)
    two = jnp.where((row == 0) | ((row == 1) & ~lower), 0.0, two)
    mine = jnp.concatenate([one, two], axis=1)
    flag = jnp.repeat(flags[:, 1:], size, axis=1)[:, :, None]
    others = jnp.concatenate(solve(targets, flag), axis=1)
    schur = trailing[0] - jnp.where(row >= 2, times_t(mine, others), 0.0)
    return mine[None], schur[None]


def solution(mesh):
    blk, col = mesh.devices.shape
    inner = Mesh(mesh.devices.reshape(blk // PLANE, PLANE, col), ("z", "p", "x"))
    rows = ("z", "p")
    in_specs = (P(None, rows, None), P(None, rows, "x"), P(), P("x"))
    out_specs = (P(None, rows, None), P(None, rows, "x"))
    return jax.shard_map(local, mesh=inner, in_specs=in_specs, out_specs=out_specs, check_vma=False)
```

```python
import jax
import jax.numpy as jnp
from jax import lax
from jax.experimental import pallas as pl
from jax.experimental.pallas import tpu as pltpu
from jax.sharding import Mesh, PartitionSpec as P

PLANE = 8
PANEL = 32
OUTER = (((0,), (0,)), ((), ()))
ROWS = (((1,), (1,)), ((), ()))


def split(x):
    high = x.astype(jnp.bfloat16)
    rest = x - high.astype(jnp.float32)
    mid = rest.astype(jnp.bfloat16)
    low = (rest - mid.astype(jnp.float32)).astype(jnp.bfloat16)
    return high, mid, low


def outer(left, right):
    a, b, c = split(left)
    h, m, l = split(right)
    return lax.dot_general(
        jnp.concatenate([a, a, b, a, b, c], axis=0),
        jnp.concatenate([h, m, h, l, m, h], axis=0),
        OUTER,
        preferred_element_type=jnp.float32,
    )


def recip(d):
    r = pl.reciprocal(d, approx=True)
    return r * (2.0 - d * r)


def lane_block(x, lo, count):
    lane = lax.broadcasted_iota(jnp.int32, x.shape, 1)
    return (lane >= lo) & (lane < lo + count)


def inverse_factor(matrix):
    n = matrix.shape[0]
    groups, tiles = PANEL // 8, n // 128
    sub = lax.broadcasted_iota(jnp.int32, (8, 128), 0)
    lane = lax.broadcasted_iota(jnp.int32, (8, 128), 1)
    rest = matrix
    done = []
    for j in range(n // PANEL):
        lo = PANEL * j
        rows, rest = rest[:PANEL], rest[PANEL:]
        tile, off = lo // 128, lo % 128
        cols = [
            [
                jnp.broadcast_to(rows[8 * g : 8 * g + 8, lo + k : lo + k + 1], (8, 128))
                if g >= k // 8
                else None
                for g in range(groups)
            ]
            for k in range(PANEL)
        ]
        u = [
            [rows[8 * g : 8 * g + 8, 128 * c : 128 * c + 128] for c in range(tiles)]
            for g in range(groups)
        ]
        for g in range(groups):
            eye = (lane - off == sub + 8 * g).astype(jnp.float32)
            u[g][tile] = jnp.where(lane_block(eye, off, PANEL), eye, u[g][tile])
        scale = [jnp.zeros((8, 128), jnp.float32)] * groups
        for k in range(PANEL):
            at, s = k // 8, k % 8
            col = cols[k]
            d = jnp.broadcast_to(col[at][s : s + 1], (8, 128))
            r = recip(d)
            scale[at] = jnp.where(sub == s, lax.rsqrt(d), scale[at])
            if k == PANEL - 1:
                break
            low = [None] * at + [jnp.where(sub > s, col[at], 0.0)] + col[at + 1 :]
            ratio = [None if x is None else x * r for x in low]
            for i in range(k + 1, PANEL):
                first = i // 8
                b = jnp.broadcast_to(col[first][i % 8 : i % 8 + 1], (8, 128))
                for g in range(first, groups):
                    if i == k + 1:
                        cols[i][g] = cols[i][g] - (low[g] * b) * r
                    else:
                        cols[i][g] = cols[i][g] - ratio[g] * b
            for c in range(tiles):
                b = jnp.broadcast_to(u[at][c][s : s + 1], (8, 128))
                for g in range(at if s < 7 else at + 1, groups):
                    u[g][c] = u[g][c] - ratio[g] * b
        u = jnp.concatenate(
            [
                jnp.concatenate([x * scale[g] for x in u[g]], axis=1)
                for g in range(groups)
            ],
            axis=0,
        )
        done.append(u)
        left = rest.shape[0]
        if left:
            update = outer(u[:, 128 * ((lo + PANEL) // 128) :], u)
            update = update[update.shape[0] - left :]
            rest = jnp.where(lane_block(rest, lo, PANEL), 0.0, rest) - update
    full = jnp.concatenate(done, axis=0)
    row = lax.broadcasted_iota(jnp.int32, full.shape, 0)
    column = lax.broadcasted_iota(jnp.int32, full.shape, 1)
    return jnp.where(row >= column, full, 0.0)


def dot6(left, right):
    a, b, c = left
    h, m, l = right
    return lax.dot_general(
        jnp.concatenate([a, a, b, a, b, c], axis=1),
        jnp.concatenate([h, m, h, l, m, h], axis=1),
        ROWS,
        preferred_element_type=jnp.float32,
    )


def dot3(left, right):
    a, b, _ = left
    h, m, _ = right
    return lax.dot_general(
        jnp.concatenate([a, a, b], axis=1),
        jnp.concatenate([h, m, h], axis=1),
        ROWS,
        preferred_element_type=jnp.float32,
    )


def flag(pattern, part, row):
    return pattern[part, row].astype(jnp.float32)


def pivot_kernel(row_ref, pattern, blocks, own, lead, below, second, mine):
    size, width = own.shape
    half = width // 2
    row = row_ref[0]
    w00 = inverse_factor(blocks[:, 0].reshape(size, half))
    lead[...] = w00
    w00 = split(w00)
    l10 = dot6(split(blocks[:, 1].reshape(size, half)), w00)
    below[...] = l10
    l10 = split(l10)
    w11 = inverse_factor(blocks[:, 2].reshape(size, half) - dot6(l10, l10))
    second[...] = w11
    w11 = split(w11)
    one = dot6(split(own[:, :half] * flag(pattern, 0, row)), w00)
    inner = own[:, half:] * flag(pattern, 1, row) - dot6(split(one), l10)
    two = dot6(split(inner), w11)
    shape = (size, half)
    upper = lax.broadcasted_iota(jnp.int32, shape, 0) < lax.broadcasted_iota(jnp.int32, shape, 1)
    mine[:, :half] = jnp.where(upper & (row == 0), 0.0, one)
    mine[:, half:] = jnp.where((upper & (row == 1)) | (row == 0), 0.0, two)


def update_kernel(row_ref, pattern, rows, targets, lead, below, second, mine, trailing, out):
    size, width = mine.shape
    half = width // 2
    w00, l10, w11 = split(lead[...]), split(below[...]), split(second[...])
    left, right = split(mine[:, :half]), split(mine[:, half:])
    keep = (row_ref[0] >= 2).astype(jnp.float32)
    for t in range(targets.shape[1]):
        block = targets[:, t].reshape(size, width)
        one = split(dot3(split(block[:, :half] * flag(pattern, 0, rows[t])), w00))
        inner = block[:, half:] * flag(pattern, 1, rows[t]) - dot3(one, l10)
        two = split(dot3(split(inner), w11))
        update = dot3(left, one) + dot3(right, two)
        at = slice(t * size, (t + 1) * size)
        out[:, at] = trailing[:, at] - keep * update


def call(kernel, scalars, arrays, shapes, flops):
    specs = [pl.BlockSpec(memory_space=pltpu.SMEM)] * len(scalars)
    specs += [pl.BlockSpec(memory_space=pltpu.VMEM)] * len(arrays)
    outs = [jax.ShapeDtypeStruct(shape, jnp.float32) for shape in shapes]
    return pl.pallas_call(
        kernel,
        in_specs=specs,
        out_specs=[pl.BlockSpec(memory_space=pltpu.VMEM)] * len(outs),
        out_shape=outs,
        compiler_params=pltpu.CompilerParams(vmem_limit_bytes=32 << 20),
        cost_estimate=pl.CostEstimate(flops=flops, bytes_accessed=1 << 20, transcendentals=0),
    )(*scalars, *arrays)


def copies(x, count):
    return jnp.broadcast_to(x[None], (count,) + x.shape)


def pick(x, at, axis):
    return lax.dynamic_index_in_dim(x, at, axis, keepdims=False)


def local(panel, trailing, pattern, target_rows):
    _, size, width = panel.shape
    half = width // 2
    nz, npl = lax.axis_size("z"), lax.axis_size("p")
    row = (lax.axis_index("z") * npl + lax.axis_index("p")).astype(jnp.int32)[None]
    count = target_rows.shape[0]
    own = panel[0]
    coarse, lanes = size // npl, width // 128
    sub = coarse * lanes // nz
    pieces = lax.all_to_all(own.reshape(npl, coarse, width), "p", 0, 0)
    chosen = [pieces[0], pieces[1]]
    chosen += [pick(pieces, target_rows[t] % npl, 0) for t in range(count)]
    wanted = len(chosen)
    chosen = jnp.stack(chosen).reshape(wanted, coarse // sub, sub, lanes, 128)
    chosen = chosen.transpose(1, 3, 0, 2, 4).reshape(nz, wanted * sub, 128)
    got = lax.all_to_all(chosen, "z", 0, 0).reshape(nz, wanted, sub, 128)
    held = [got[0, 0], got[0, 1]]
    held += [pick(got[:, 2 + t], target_rows[t] // npl, 0) for t in range(count)]
    held = lax.all_to_all(copies(jnp.concatenate(held), nz), "z", 0, 0)
    held = held.reshape(coarse // sub, lanes, wanted, sub, 128).transpose(2, 0, 3, 1, 4)
    held = held.reshape(wanted, coarse, width)
    blocks = jnp.stack([held[0, :, :half], held[1, :, :half], held[1, :, half:]])
    blocks = lax.all_to_all(copies(blocks, npl), "p", 0, 0)
    targets = lax.all_to_all(copies(held[2:], npl), "p", 0, 0)
    square = (size, half)
    lead, below, second, mine = call(
        pivot_kernel,
        (row, pattern),
        (blocks, own),
        (square, square, square, (size, width)),
        1 << 34,
    )
    (schur,) = call(
        update_kernel,
        (row, pattern, target_rows),
        (targets, lead, below, second, mine, trailing[0]),
        ((size, trailing.shape[2]),),
        1 << 30,
    )
    return mine[None], schur[None]


def solution(mesh):
    blk, col = mesh.devices.shape
    inner = Mesh(mesh.devices.reshape(blk // PLANE, PLANE, col), ("z", "p", "x"))
    rows = ("z", "p")
    in_specs = (P(None, rows, None), P(None, rows, "x"), P(), P("x"))
    out_specs = (P(None, rows, None), P(None, rows, "x"))
    return jax.shard_map(local, mesh=inner, in_specs=in_specs, out_specs=out_specs, check_vma=False)
```

```python
import jax
import jax.numpy as jnp
from jax import lax
from jax.experimental import pallas as pl
from jax.experimental.pallas import tpu as pltpu
from jax.sharding import Mesh, PartitionSpec as P

PLANE = 8
PANEL = 32
OUTER = (((0,), (0,)), ((), ()))
ROWS = (((1,), (1,)), ((), ()))


def split(x):
    high = x.astype(jnp.bfloat16)
    rest = x - high.astype(jnp.float32)
    mid = rest.astype(jnp.bfloat16)
    low = (rest - mid.astype(jnp.float32)).astype(jnp.bfloat16)
    return high, mid, low


def outer(left, right):
    a, b, c = split(left)
    h, m, l = split(right)
    return lax.dot_general(
        jnp.concatenate([a, a, b, a, b, c], axis=0),
        jnp.concatenate([h, m, h, l, m, h], axis=0),
        OUTER,
        preferred_element_type=jnp.float32,
    )


def recip(d):
    r = pl.reciprocal(d, approx=True)
    return r * (2.0 - d * r)


def lane_block(x, lo, count):
    lane = lax.broadcasted_iota(jnp.int32, x.shape, 1)
    return (lane >= lo) & (lane < lo + count)


def inverse_factor(matrix):
    n = matrix.shape[0]
    groups, tiles = PANEL // 8, n // 128
    sub = lax.broadcasted_iota(jnp.int32, (8, 128), 0)
    lane = lax.broadcasted_iota(jnp.int32, (8, 128), 1)
    rest = matrix
    done = []
    for j in range(n // PANEL):
        lo = PANEL * j
        rows, rest = rest[:PANEL], rest[PANEL:]
        tile, off = lo // 128, lo % 128
        cols = [
            [
                jnp.broadcast_to(rows[8 * g : 8 * g + 8, lo + k : lo + k + 1], (8, 128))
                if g >= k // 8
                else None
                for g in range(groups)
            ]
            for k in range(PANEL)
        ]
        u = [
            [rows[8 * g : 8 * g + 8, 128 * c : 128 * c + 128] for c in range(tiles)]
            for g in range(groups)
        ]
        for g in range(groups):
            eye = (lane - off == sub + 8 * g).astype(jnp.float32)
            u[g][tile] = jnp.where(lane_block(eye, off, PANEL), eye, u[g][tile])
        scale = [jnp.zeros((8, 128), jnp.float32)] * groups
        for k in range(PANEL):
            at, s = k // 8, k % 8
            col = cols[k]
            d = jnp.broadcast_to(col[at][s : s + 1], (8, 128))
            r = recip(d)
            scale[at] = jnp.where(sub == s, lax.rsqrt(d), scale[at])
            if k == PANEL - 1:
                break
            low = [None] * at + [jnp.where(sub > s, col[at], 0.0)] + col[at + 1 :]
            ratio = [None if x is None else x * r for x in low]
            for i in range(k + 1, PANEL):
                first = i // 8
                b = jnp.broadcast_to(col[first][i % 8 : i % 8 + 1], (8, 128))
                for g in range(first, groups):
                    if i == k + 1:
                        cols[i][g] = cols[i][g] - (low[g] * b) * r
                    else:
                        cols[i][g] = cols[i][g] - ratio[g] * b
            for c in range(tiles):
                b = jnp.broadcast_to(u[at][c][s : s + 1], (8, 128))
                for g in range(at if s < 7 else at + 1, groups):
                    u[g][c] = u[g][c] - ratio[g] * b
        u = jnp.concatenate(
            [
                jnp.concatenate([x * scale[g] for x in u[g]], axis=1)
                for g in range(groups)
            ],
            axis=0,
        )
        done.append(u)
        left = rest.shape[0]
        if left:
            update = outer(u[:, 128 * ((lo + PANEL) // 128) :], u)
            update = update[update.shape[0] - left :]
            rest = jnp.where(lane_block(rest, lo, PANEL), 0.0, rest) - update
    full = jnp.concatenate(done, axis=0)
    row = lax.broadcasted_iota(jnp.int32, full.shape, 0)
    column = lax.broadcasted_iota(jnp.int32, full.shape, 1)
    return jnp.where(row >= column, full, 0.0)


def dot6(left, right):
    a, b, c = left
    h, m, l = right
    return lax.dot_general(
        jnp.concatenate([a, a, b, a, b, c], axis=1),
        jnp.concatenate([h, m, h, l, m, h], axis=1),
        ROWS,
        preferred_element_type=jnp.float32,
    )


def dot3(left, right):
    a, b, _ = left
    h, m, _ = right
    return lax.dot_general(
        jnp.concatenate([a, a, b], axis=1),
        jnp.concatenate([h, m, h], axis=1),
        ROWS,
        preferred_element_type=jnp.float32,
    )


def flag(pattern, part, row):
    return pattern[part, row].astype(jnp.float32)


def pivot_kernel(blocks, solver):
    size, half = solver.shape[1:]
    w00 = inverse_factor(blocks[:, 0].reshape(size, half))
    solver[0] = w00
    l10 = dot6(split(blocks[:, 1].reshape(size, half)), split(w00))
    solver[1] = l10
    l10 = split(l10)
    solver[2] = inverse_factor(blocks[:, 2].reshape(size, half) - dot6(l10, l10))


def own_kernel(row_ref, pattern, own, solver, mine):
    size, width = own.shape
    half = width // 2
    row = row_ref[0]
    w00, l10, w11 = split(solver[0]), split(solver[1]), split(solver[2])
    one = dot6(split(own[:, :half] * flag(pattern, 0, row)), w00)
    inner = own[:, half:] * flag(pattern, 1, row) - dot6(split(one), l10)
    two = dot6(split(inner), w11)
    shape = (size, half)
    upper = lax.broadcasted_iota(jnp.int32, shape, 0) < lax.broadcasted_iota(jnp.int32, shape, 1)
    mine[:, :half] = jnp.where(upper & (row == 0), 0.0, one)
    mine[:, half:] = jnp.where((upper & (row == 1)) | (row == 0), 0.0, two)


def update_kernel(row_ref, pattern, rows, targets, solver, mine, trailing, out):
    size, width = mine.shape
    half = width // 2
    w00, l10, w11 = split(solver[0]), split(solver[1]), split(solver[2])
    left, right = split(mine[:, :half]), split(mine[:, half:])
    keep = (row_ref[0] >= 2).astype(jnp.float32)
    for t in range(targets.shape[1]):
        block = targets[:, t].reshape(size, width)
        one = split(dot3(split(block[:, :half] * flag(pattern, 0, rows[t])), w00))
        inner = block[:, half:] * flag(pattern, 1, rows[t]) - dot3(one, l10)
        two = split(dot3(split(inner), w11))
        update = dot3(left, one) + dot3(right, two)
        at = slice(t * size, (t + 1) * size)
        out[:, at] = trailing[:, at] - keep * update


def call(kernel, scalars, arrays, shape, flops, vmem=12):
    specs = [pl.BlockSpec(memory_space=pltpu.SMEM)] * len(scalars)
    specs += [pl.BlockSpec(memory_space=pltpu.VMEM)] * len(arrays)
    return pl.pallas_call(
        kernel,
        in_specs=specs,
        out_specs=pl.BlockSpec(memory_space=pltpu.VMEM),
        out_shape=jax.ShapeDtypeStruct(shape, jnp.float32),
        compiler_params=pltpu.CompilerParams(vmem_limit_bytes=vmem << 20),
        cost_estimate=pl.CostEstimate(flops=flops, bytes_accessed=1 << 20, transcendentals=0),
    )(*scalars, *arrays)


def copies(x, count):
    return jnp.broadcast_to(x[None], (count,) + x.shape)


def pick(x, at, axis):
    return lax.dynamic_index_in_dim(x, at, axis, keepdims=False)


def local(panel, trailing, pattern, target_rows):
    _, size, width = panel.shape
    half = width // 2
    nz, npl, nx = lax.axis_size("z"), lax.axis_size("p"), lax.axis_size("x")
    row = (lax.axis_index("z") * npl + lax.axis_index("p")).astype(jnp.int32)[None]
    count = target_rows.shape[0]
    own = panel[0]
    fine, lanes = size // (npl * nx), width // 128
    sub = fine * lanes // nz
    shares = npl * nx
    everyone = lax.all_gather(target_rows, "x", axis=0, tiled=True)
    pieces = pick(own.reshape(npl, nx, fine, width), lax.axis_index("x"), 1)
    pieces = pieces.reshape(npl, fine // sub, sub, lanes, 128).transpose(1, 3, 0, 2, 4)
    pieces = lax.all_to_all(pieces.reshape(nz * npl, sub, 128), ("z", "p"), 0, 0)
    held = jnp.concatenate(
        [pieces[:2]]
        + [lax.dynamic_slice_in_dim(pieces, everyone[t], 1, 0) for t in range(count * nx)]
    )
    wanted = held.shape[0]
    held = lax.all_to_all(copies(held.reshape(wanted * sub, 128), nz), "z", 0, 0)
    held = held.reshape(fine // sub, lanes, wanted, sub, 128).transpose(2, 0, 3, 1, 4)
    held = held.reshape(wanted, fine, width)
    blocks = jnp.stack([held[0, :, :half], held[1, :, :half], held[1, :, half:]])
    blocks = lax.all_to_all(copies(blocks, shares), ("p", "x"), 0, 0)
    targets = copies(held[2:].reshape(nx, count, fine, width), npl)
    targets = targets.reshape(shares, count, fine, width)
    targets = lax.all_to_all(targets, ("p", "x"), 0, 0)
    solver = call(pivot_kernel, (), (blocks,), (3, size, half), 1 << 34, 16)
    mine = call(own_kernel, (row, pattern), (own, solver), (size, width), 1 << 30)
    schur = call(
        update_kernel,
        (row, pattern, target_rows),
        (targets, solver, mine, trailing[0]),
        (size, trailing.shape[2]),
        1 << 30,
    )
    return mine[None], schur[None]


def solution(mesh):
    blk, col = mesh.devices.shape
    inner = Mesh(mesh.devices.reshape(blk // PLANE, PLANE, col), ("z", "p", "x"))
    rows = ("z", "p")
    in_specs = (P(None, rows, None), P(None, rows, "x"), P(), P("x"))
    out_specs = (P(None, rows, None), P(None, rows, "x"))
    return jax.shard_map(local, mesh=inner, in_specs=in_specs, out_specs=out_specs, check_vma=False)
```

```python
import jax
import jax.numpy as jnp
from jax import lax
from jax.experimental import pallas as pl
from jax.experimental.pallas import tpu as pltpu
from jax.sharding import Mesh, PartitionSpec as P

PLANE = 8
PANEL = 32
OUTER = (((0,), (0,)), ((), ()))
ROWS = (((1,), (1,)), ((), ()))


def split(x):
    high = x.astype(jnp.bfloat16)
    rest = x - high.astype(jnp.float32)
    mid = rest.astype(jnp.bfloat16)
    low = (rest - mid.astype(jnp.float32)).astype(jnp.bfloat16)
    return high, mid, low


def outer(left, right):
    a, b, c = split(left)
    h, m, l = split(right)
    return lax.dot_general(
        jnp.concatenate([a, a, b, a, b, c], axis=0),
        jnp.concatenate([h, m, h, l, m, h], axis=0),
        OUTER,
        preferred_element_type=jnp.float32,
    )


def recip(d):
    r = pl.reciprocal(d, approx=True)
    return r * (2.0 - d * r)


def lane_block(x, lo, count):
    lane = lax.broadcasted_iota(jnp.int32, x.shape, 1)
    return (lane >= lo) & (lane < lo + count)


def inverse_factor(matrix):
    n = matrix.shape[0]
    groups, tiles = PANEL // 8, n // 128
    sub = lax.broadcasted_iota(jnp.int32, (8, 128), 0)
    lane = lax.broadcasted_iota(jnp.int32, (8, 128), 1)
    rest = matrix
    done = []
    for j in range(n // PANEL):
        lo = PANEL * j
        rows, rest = rest[:PANEL], rest[PANEL:]
        tile, off = lo // 128, lo % 128
        cols = [
            [
                jnp.broadcast_to(rows[8 * g : 8 * g + 8, lo + k : lo + k + 1], (8, 128))
                if g >= k // 8
                else None
                for g in range(groups)
            ]
            for k in range(PANEL)
        ]
        u = [
            [rows[8 * g : 8 * g + 8, 128 * c : 128 * c + 128] for c in range(tiles)]
            for g in range(groups)
        ]
        for g in range(groups):
            eye = (lane - off == sub + 8 * g).astype(jnp.float32)
            u[g][tile] = jnp.where(lane_block(eye, off, PANEL), eye, u[g][tile])
        scale = [jnp.zeros((8, 128), jnp.float32)] * groups
        for k in range(PANEL):
            at, s = k // 8, k % 8
            col = cols[k]
            d = jnp.broadcast_to(col[at][s : s + 1], (8, 128))
            r = recip(d)
            scale[at] = jnp.where(sub == s, lax.rsqrt(d), scale[at])
            if k == PANEL - 1:
                break
            low = [None] * at + [jnp.where(sub > s, col[at], 0.0)] + col[at + 1 :]
            ratio = [None if x is None else x * r for x in low]
            for i in range(k + 1, PANEL):
                first = i // 8
                b = jnp.broadcast_to(col[first][i % 8 : i % 8 + 1], (8, 128))
                for g in range(first, groups):
                    if i == k + 1:
                        cols[i][g] = cols[i][g] - (low[g] * b) * r
                    else:
                        cols[i][g] = cols[i][g] - ratio[g] * b
            for c in range(tiles):
                b = jnp.broadcast_to(u[at][c][s : s + 1], (8, 128))
                for g in range(at if s < 7 else at + 1, groups):
                    u[g][c] = u[g][c] - ratio[g] * b
        u = jnp.concatenate(
            [
                jnp.concatenate([x * scale[g] for x in u[g]], axis=1)
                for g in range(groups)
            ],
            axis=0,
        )
        done.append(u)
        left = rest.shape[0]
        if left:
            update = outer(u[:, 128 * ((lo + PANEL) // 128) :], u)
            update = update[update.shape[0] - left :]
            rest = jnp.where(lane_block(rest, lo, PANEL), 0.0, rest) - update
    full = jnp.concatenate(done, axis=0)
    row = lax.broadcasted_iota(jnp.int32, full.shape, 0)
    column = lax.broadcasted_iota(jnp.int32, full.shape, 1)
    return jnp.where(row >= column, full, 0.0)


def dot6(left, right):
    a, b, c = left
    h, m, l = right
    return lax.dot_general(
        jnp.concatenate([a, a, b, a, b, c], axis=1),
        jnp.concatenate([h, m, h, l, m, h], axis=1),
        ROWS,
        preferred_element_type=jnp.float32,
    )


def dot3(left, right):
    a, b, _ = left
    h, m, _ = right
    return lax.dot_general(
        jnp.concatenate([a, a, b], axis=1),
        jnp.concatenate([h, m, h], axis=1),
        ROWS,
        preferred_element_type=jnp.float32,
    )


def flag(pattern, part, row):
    return pattern[part, row].astype(jnp.float32)


def pivot_kernel(blocks, solver):
    size, half = solver.shape[1:]
    w00 = inverse_factor(blocks[:, 0].reshape(size, half))
    solver[0] = w00
    l10 = dot6(split(blocks[:, 1].reshape(size, half)), split(w00))
    solver[1] = l10
    l10 = split(l10)
    solver[2] = inverse_factor(blocks[:, 2].reshape(size, half) - dot6(l10, l10))


def own_kernel(row_ref, pattern, own, solver, mine):
    size, width = own.shape
    half = width // 2
    row = row_ref[0]
    w00, l10, w11 = split(solver[0]), split(solver[1]), split(solver[2])
    one = dot6(split(own[:, :half] * flag(pattern, 0, row)), w00)
    inner = own[:, half:] * flag(pattern, 1, row) - dot6(split(one), l10)
    two = dot6(split(inner), w11)
    shape = (size, half)
    upper = lax.broadcasted_iota(jnp.int32, shape, 0) < lax.broadcasted_iota(jnp.int32, shape, 1)
    mine[:, :half] = jnp.where(upper & (row == 0), 0.0, one)
    mine[:, half:] = jnp.where((upper & (row == 1)) | (row == 0), 0.0, two)


def update_kernel(row_ref, pattern, rows, targets, solver, mine, trailing, out):
    size, width = mine.shape
    half = width // 2
    w00, l10, w11 = split(solver[0]), split(solver[1]), split(solver[2])
    left, right = split(mine[:, :half]), split(mine[:, half:])
    keep = (row_ref[0] >= 2).astype(jnp.float32)
    for t in range(targets.shape[1]):
        block = targets[:, t].reshape(size, width)
        one = split(dot3(split(block[:, :half] * flag(pattern, 0, rows[t])), w00))
        inner = block[:, half:] * flag(pattern, 1, rows[t]) - dot3(one, l10)
        two = split(dot3(split(inner), w11))
        update = dot3(left, one) + dot3(right, two)
        at = slice(t * size, (t + 1) * size)
        out[:, at] = trailing[:, at] - keep * update


def call(kernel, scalars, arrays, shape, flops, vmem=12):
    specs = [pl.BlockSpec(memory_space=pltpu.SMEM)] * len(scalars)
    specs += [pl.BlockSpec(memory_space=pltpu.VMEM)] * len(arrays)
    return pl.pallas_call(
        kernel,
        in_specs=specs,
        out_specs=pl.BlockSpec(memory_space=pltpu.VMEM),
        out_shape=jax.ShapeDtypeStruct(shape, jnp.float32),
        compiler_params=pltpu.CompilerParams(vmem_limit_bytes=vmem << 20),
        cost_estimate=pl.CostEstimate(flops=flops, bytes_accessed=1 << 20, transcendentals=0),
    )(*scalars, *arrays)


def copies(x, count):
    return jnp.broadcast_to(x[None], (count,) + x.shape)


def pick(x, at, axis):
    return lax.dynamic_index_in_dim(x, at, axis, keepdims=False)


def local(panel, trailing, pattern, target_rows):
    _, size, width = panel.shape
    half = width // 2
    nz, npl, nx = lax.axis_size("z"), lax.axis_size("p"), lax.axis_size("x")
    row = (lax.axis_index("z") * npl + lax.axis_index("p")).astype(jnp.int32)[None]
    count = target_rows.shape[0]
    own = panel[0]
    fine, coarse = size // (npl * nx), size // npl
    pieces = lax.all_to_all(own.reshape(npl, coarse, width), "p", 0, 0)
    chosen = jnp.stack([pick(pieces, target_rows[t] % npl, 0) for t in range(count)])
    chosen, pieces = lax.optimization_barrier((chosen, pieces))
    planes = lax.all_gather(chosen, "z", axis=0)
    share = lax.dynamic_slice_in_dim(pieces[:2], lax.axis_index("x") * fine, fine, 1)
    share = jnp.stack([share[0, :, :half], share[1, :, :half], share[1, :, half:]])
    share = lax.all_to_all(copies(share, nz), "z", 0, 0)[0]
    blocks = lax.all_to_all(copies(share, npl * nx), ("p", "x"), 0, 0)
    solver = call(pivot_kernel, (), (blocks,), (3, size, half), 1 << 34, 16)
    planes, solver = lax.optimization_barrier((planes, solver))
    held = jnp.concatenate(
        [
            lax.dynamic_slice(planes, (target_rows[t] // npl, t, 0, 0), (1, 1, coarse, width))
            for t in range(count)
        ],
        axis=1,
    )[0]
    targets = lax.all_to_all(copies(held, npl), "p", 0, 0)
    mine = call(own_kernel, (row, pattern), (own, solver), (size, width), 1 << 30)
    schur = call(
        update_kernel,
        (row, pattern, target_rows),
        (targets, solver, mine, trailing[0]),
        (size, trailing.shape[2]),
        1 << 30,
    )
    return mine[None], schur[None]


def solution(mesh):
    blk, col = mesh.devices.shape
    inner = Mesh(mesh.devices.reshape(blk // PLANE, PLANE, col), ("z", "p", "x"))
    rows = ("z", "p")
    in_specs = (P(None, rows, None), P(None, rows, "x"), P(), P("x"))
    out_specs = (P(None, rows, None), P(None, rows, "x"))
    return jax.shard_map(local, mesh=inner, in_specs=in_specs, out_specs=out_specs, check_vma=False)
```

```python
import jax
import jax.numpy as jnp
from jax import lax
from jax.experimental import pallas as pl
from jax.experimental.pallas import tpu as pltpu
from jax.sharding import Mesh, PartitionSpec as P

LINES, CORES = 4, 2
PANEL = 32
OUTER = (((0,), (0,)), ((), ()))
ROWS = (((1,), (1,)), ((), ()))


def split(x):
    high = x.astype(jnp.bfloat16)
    rest = x - high.astype(jnp.float32)
    mid = rest.astype(jnp.bfloat16)
    low = (rest - mid.astype(jnp.float32)).astype(jnp.bfloat16)
    return high, mid, low


def outer(left, right):
    a, b, c = split(left)
    h, m, l = split(right)
    return lax.dot_general(
        jnp.concatenate([a, a, b, a, b, c], axis=0),
        jnp.concatenate([h, m, h, l, m, h], axis=0),
        OUTER,
        preferred_element_type=jnp.float32,
    )


def lane_block(x, lo, count):
    lane = lax.broadcasted_iota(jnp.int32, x.shape, 1)
    return (lane >= lo) & (lane < lo + count)


def inverse_factor(matrix):
    n = matrix.shape[0]
    groups, tiles = PANEL // 8, n // 128
    sub = lax.broadcasted_iota(jnp.int32, (8, 128), 0)
    lane = lax.broadcasted_iota(jnp.int32, (8, 128), 1)
    rest = matrix
    done = []
    for j in range(n // PANEL):
        lo = PANEL * j
        rows, rest = rest[:PANEL], rest[PANEL:]
        tile, off = lo // 128, lo % 128
        cols = [
            [
                jnp.broadcast_to(rows[8 * g : 8 * g + 8, lo + k : lo + k + 1], (8, 128))
                if g >= k // 8
                else None
                for g in range(groups)
            ]
            for k in range(PANEL)
        ]
        u = [
            [rows[8 * g : 8 * g + 8, 128 * c : 128 * c + 128] for c in range(tiles)]
            for g in range(groups)
        ]
        for g in range(groups):
            eye = (lane - off == sub + 8 * g).astype(jnp.float32)
            u[g][tile] = jnp.where(lane_block(eye, off, PANEL), eye, u[g][tile])
        scale = [jnp.zeros((8, 128), jnp.float32)] * groups
        for k in range(PANEL):
            at, s = k // 8, k % 8
            col = cols[k]
            d = jnp.broadcast_to(col[at][s : s + 1], (8, 128))
            r = pl.reciprocal(d, approx=True)
            scale[at] = jnp.where(sub == s, lax.rsqrt(d), scale[at])
            if k == PANEL - 1:
                break
            low = [None] * at + [jnp.where(sub > s, col[at], 0.0)] + col[at + 1 :]
            ratio = [None if x is None else x * r for x in low]
            for i in range(k + 1, PANEL):
                first = i // 8
                b = jnp.broadcast_to(col[first][i % 8 : i % 8 + 1], (8, 128))
                for g in range(first, groups):
                    if i == k + 1:
                        cols[i][g] = cols[i][g] - (low[g] * b) * r
                    else:
                        cols[i][g] = cols[i][g] - ratio[g] * b
            for c in range(tiles):
                b = jnp.broadcast_to(u[at][c][s : s + 1], (8, 128))
                for g in range(at if s < 7 else at + 1, groups):
                    u[g][c] = u[g][c] - ratio[g] * b
        u = jnp.concatenate(
            [
                jnp.concatenate([x * scale[g] for x in u[g]], axis=1)
                for g in range(groups)
            ],
            axis=0,
        )
        done.append(u)
        left = rest.shape[0]
        if left:
            update = outer(u[:, 128 * ((lo + PANEL) // 128) :], u)
            update = update[update.shape[0] - left :]
            rest = jnp.where(lane_block(rest, lo, PANEL), 0.0, rest) - update
    full = jnp.concatenate(done, axis=0)
    row = lax.broadcasted_iota(jnp.int32, full.shape, 0)
    column = lax.broadcasted_iota(jnp.int32, full.shape, 1)
    return jnp.where(row >= column, full, 0.0)


def dot6(left, right):
    a, b, c = left
    h, m, l = right
    return lax.dot_general(
        jnp.concatenate([a, a, b, a, b, c], axis=1),
        jnp.concatenate([h, m, h, l, m, h], axis=1),
        ROWS,
        preferred_element_type=jnp.float32,
    )


def dot3(left, right):
    a, b, _ = left
    h, m, _ = right
    return lax.dot_general(
        jnp.concatenate([a, a, b], axis=1),
        jnp.concatenate([h, m, h], axis=1),
        ROWS,
        preferred_element_type=jnp.float32,
    )


def flag(pattern, part, row):
    return pattern[part, row].astype(jnp.float32)


def pivot_kernel(blocks, solver):
    size, half = solver.shape[1:]
    cores, lines = blocks.shape[:2]

    def gather(k):
        return jnp.concatenate([blocks[c, y, k] for y in range(lines) for c in range(cores)])

    w00 = inverse_factor(gather(0))
    solver[0] = w00
    l10 = dot6(split(gather(1)), split(w00))
    solver[1] = l10
    l10 = split(l10)
    solver[2] = inverse_factor(gather(2) - dot6(l10, l10))


def update_kernel(row_ref, pattern, rows, targets, solver, own, trailing, mine, out):
    size, width = own.shape
    half = width // 2
    row = row_ref[0]
    w00, l10, w11 = split(solver[0]), split(solver[1]), split(solver[2])
    one = dot6(split(own[:, :half] * flag(pattern, 0, row)), w00)
    inner = own[:, half:] * flag(pattern, 1, row) - dot6(split(one), l10)
    two = dot6(split(inner), w11)
    shape = (size, half)
    upper = lax.broadcasted_iota(jnp.int32, shape, 0) < lax.broadcasted_iota(jnp.int32, shape, 1)
    one = jnp.where(upper & (row == 0), 0.0, one)
    two = jnp.where((upper & (row == 1)) | (row == 0), 0.0, two)
    mine[:, :half] = one
    mine[:, half:] = two
    left, right = split(one), split(two)
    keep = (row >= 2).astype(jnp.float32)
    for t in range(targets.shape[1]):
        block = targets[:, t].reshape(size, width)
        one = split(dot3(split(block[:, :half] * flag(pattern, 0, rows[t])), w00))
        inner = block[:, half:] * flag(pattern, 1, rows[t]) - dot3(one, l10)
        two = split(dot3(split(inner), w11))
        update = dot3(left, one) + dot3(right, two)
        at = slice(t * size, (t + 1) * size)
        out[:, at] = trailing[:, at] - keep * update


def call(kernel, scalars, arrays, shapes, flops):
    specs = [pl.BlockSpec(memory_space=pltpu.SMEM)] * len(scalars)
    specs += [pl.BlockSpec(memory_space=pltpu.VMEM)] * len(arrays)
    return pl.pallas_call(
        kernel,
        in_specs=specs,
        out_specs=[pl.BlockSpec(memory_space=pltpu.VMEM)] * len(shapes),
        out_shape=[jax.ShapeDtypeStruct(shape, jnp.float32) for shape in shapes],
        compiler_params=pltpu.CompilerParams(vmem_limit_bytes=16 << 20),
        cost_estimate=pl.CostEstimate(flops=flops, bytes_accessed=1 << 20, transcendentals=0),
    )(*scalars, *arrays)


def copies(x, count):
    return jnp.broadcast_to(x[None], (count,) + x.shape)


def pick(x, at, axis):
    return lax.dynamic_index_in_dim(x, at, axis, keepdims=False)


def local(panel, trailing, pattern, target_rows):
    _, size, width = panel.shape
    half = width // 2
    plane = ("y", "core")
    nz, npl = lax.axis_size("z"), lax.axis_size(plane)
    row = (lax.axis_index("z") * npl + lax.axis_index(plane)).astype(jnp.int32)[None]
    count = target_rows.shape[0]
    own = panel[0]
    coarse, lanes = size // npl, width // 128
    sub = coarse * lanes // nz
    pieces = lax.all_to_all(own.reshape(npl, coarse, width), plane, 0, 0)
    chosen = [pieces[0], pieces[1]]
    chosen += [pick(pieces, target_rows[t] % npl, 0) for t in range(count)]
    wanted = len(chosen)
    chosen = jnp.stack(chosen).reshape(wanted, coarse // sub, sub, lanes, 128)
    chosen = chosen.transpose(1, 3, 0, 2, 4).reshape(nz, wanted * sub, 128)
    got = lax.all_to_all(chosen, "z", 0, 0).reshape(nz, wanted, sub, 128)
    held = [got[0, 0], got[0, 1]]
    held += [pick(got[:, 2 + t], target_rows[t] // npl, 0) for t in range(count)]
    held = lax.all_to_all(copies(jnp.concatenate(held), nz), "z", 0, 0)
    held = held.reshape(coarse // sub, lanes, wanted, sub, 128).transpose(2, 0, 3, 1, 4)
    held = held.reshape(wanted, coarse, width)
    blocks = jnp.stack([held[0, :, :half], held[1, :, :half], held[1, :, half:]])
    blocks = lax.all_to_all(copies(blocks, lax.axis_size("y")), "y", 0, 0)
    blocks = lax.all_gather(blocks, "core", axis=0)
    targets = lax.all_to_all(copies(held[2:], npl), plane, 0, 0)
    (solver,) = call(pivot_kernel, (), (blocks,), ((3, size, half),), 1 << 34)
    mine, schur = call(
        update_kernel,
        (row, pattern, target_rows),
        (targets, solver, own, trailing[0]),
        ((size, width), (size, trailing.shape[2])),
        1 << 30,
    )
    return mine[None], schur[None]


def solution(mesh):
    blk, col = mesh.devices.shape
    inner = mesh.devices.reshape(blk // (LINES * CORES), LINES, CORES, col)
    inner = Mesh(inner, ("z", "y", "core", "x"))
    rows = ("z", "y", "core")
    in_specs = (P(None, rows, None), P(None, rows, "x"), P(), P("x"))
    out_specs = (P(None, rows, None), P(None, rows, "x"))
    return jax.shard_map(local, mesh=inner, in_specs=in_specs, out_specs=out_specs, check_vma=False)
```

```python
import jax
import jax.numpy as jnp
from jax import lax
from jax.experimental import pallas as pl
from jax.experimental.pallas import tpu as pltpu
from jax.sharding import Mesh, PartitionSpec as P

LINES, CORES = 4, 2
PANEL = 32
OUTER = (((0,), (0,)), ((), ()))
ROWS = (((1,), (1,)), ((), ()))


def split(x):
    high = x.astype(jnp.bfloat16)
    rest = x - high.astype(jnp.float32)
    mid = rest.astype(jnp.bfloat16)
    low = (rest - mid.astype(jnp.float32)).astype(jnp.bfloat16)
    return high, mid, low


def outer(left, right):
    a, b, c = split(left)
    h, m, l = split(right)
    return lax.dot_general(
        jnp.concatenate([a, a, b, a, b, c], axis=0),
        jnp.concatenate([h, m, h, l, m, h], axis=0),
        OUTER,
        preferred_element_type=jnp.float32,
    )


def lane_block(x, lo, count):
    lane = lax.broadcasted_iota(jnp.int32, x.shape, 1)
    return (lane >= lo) & (lane < lo + count)


def inverse_factor(matrix):
    n = matrix.shape[0]
    groups, tiles = PANEL // 8, n // 128
    sub = lax.broadcasted_iota(jnp.int32, (8, 128), 0)
    lane = lax.broadcasted_iota(jnp.int32, (8, 128), 1)
    rest = matrix
    done = []
    for j in range(n // PANEL):
        lo = PANEL * j
        rows, rest = rest[:PANEL], rest[PANEL:]
        tile, off = lo // 128, lo % 128
        cols = [
            [
                jnp.broadcast_to(rows[8 * g : 8 * g + 8, lo + k : lo + k + 1], (8, 128))
                if g >= k // 8
                else None
                for g in range(groups)
            ]
            for k in range(PANEL)
        ]
        u = [
            [rows[8 * g : 8 * g + 8, 128 * c : 128 * c + 128] for c in range(tiles)]
            for g in range(groups)
        ]
        for g in range(groups):
            eye = (lane - off == sub + 8 * g).astype(jnp.float32)
            u[g][tile] = jnp.where(lane_block(eye, off, PANEL), eye, u[g][tile])
        scale = [jnp.zeros((8, 128), jnp.float32)] * groups
        for k in range(PANEL):
            at, s = k // 8, k % 8
            col = cols[k]
            d = jnp.broadcast_to(col[at][s : s + 1], (8, 128))
            r = pl.reciprocal(d, approx=True)
            scale[at] = jnp.where(sub == s, lax.rsqrt(d), scale[at])
            if k == PANEL - 1:
                break
            low = [None] * at + [jnp.where(sub > s, col[at], 0.0)] + col[at + 1 :]
            ratio = [None if x is None else x * r for x in low]
            for i in range(k + 1, PANEL):
                first = i // 8
                b = jnp.broadcast_to(col[first][i % 8 : i % 8 + 1], (8, 128))
                for g in range(first, groups):
                    if i == k + 1:
                        cols[i][g] = cols[i][g] - (low[g] * b) * r
                    else:
                        cols[i][g] = cols[i][g] - ratio[g] * b
            for c in range(tiles):
                b = jnp.broadcast_to(u[at][c][s : s + 1], (8, 128))
                for g in range(at if s < 7 else at + 1, groups):
                    u[g][c] = u[g][c] - ratio[g] * b
        u = jnp.concatenate(
            [
                jnp.concatenate([x * scale[g] for x in u[g]], axis=1)
                for g in range(groups)
            ],
            axis=0,
        )
        done.append(u)
        left = rest.shape[0]
        if left:
            update = outer(u[:, 128 * ((lo + PANEL) // 128) :], u)
            update = update[update.shape[0] - left :]
            rest = jnp.where(lane_block(rest, lo, PANEL), 0.0, rest) - update
    full = jnp.concatenate(done, axis=0)
    row = lax.broadcasted_iota(jnp.int32, full.shape, 0)
    column = lax.broadcasted_iota(jnp.int32, full.shape, 1)
    return jnp.where(row >= column, full, 0.0)


def dot6(left, right):
    a, b, c = left
    h, m, l = right
    return lax.dot_general(
        jnp.concatenate([a, a, b, a, b, c], axis=1),
        jnp.concatenate([h, m, h, l, m, h], axis=1),
        ROWS,
        preferred_element_type=jnp.float32,
    )


def dot3(left, right):
    a, b, _ = left
    h, m, _ = right
    return lax.dot_general(
        jnp.concatenate([a, a, b], axis=1),
        jnp.concatenate([h, m, h], axis=1),
        ROWS,
        preferred_element_type=jnp.float32,
    )


def flag(pattern, part, row):
    return pattern[part, row].astype(jnp.float32)


def pivot_kernel(blocks, solver):
    size, half = solver.shape[1:]
    cores, lines, planes = blocks.shape[:3]

    def gather(k):
        rows = [
            [blocks[c, y, x, 2 * k + i] for i in range(2)]
            for y in range(lines)
            for c in range(cores)
            for x in range(planes)
        ]
        return jnp.concatenate([jnp.concatenate(tiles, axis=1) for tiles in rows])

    w00 = inverse_factor(gather(0))
    solver[0] = w00
    l10 = dot6(split(gather(1)), split(w00))
    solver[1] = l10
    l10 = split(l10)
    solver[2] = inverse_factor(gather(2) - dot6(l10, l10))


def update_kernel(row_ref, pattern, rows, targets, solver, own, trailing, mine, out):
    size, width = own.shape
    half = width // 2
    row = row_ref[0]
    w00, l10, w11 = split(solver[0]), split(solver[1]), split(solver[2])
    one = dot6(split(own[:, :half] * flag(pattern, 0, row)), w00)
    inner = own[:, half:] * flag(pattern, 1, row) - dot6(split(one), l10)
    two = dot6(split(inner), w11)
    shape = (size, half)
    upper = lax.broadcasted_iota(jnp.int32, shape, 0) < lax.broadcasted_iota(jnp.int32, shape, 1)
    one = jnp.where(upper & (row == 0), 0.0, one)
    two = jnp.where((upper & (row == 1)) | (row == 0), 0.0, two)
    mine[:, :half] = one
    mine[:, half:] = two
    left, right = split(one), split(two)
    keep = (row >= 2).astype(jnp.float32)
    for t in range(targets.shape[1]):
        block = targets[:, t].reshape(size, width)
        one = split(dot3(split(block[:, :half] * flag(pattern, 0, rows[t])), w00))
        inner = block[:, half:] * flag(pattern, 1, rows[t]) - dot3(one, l10)
        two = split(dot3(split(inner), w11))
        update = dot3(left, one) + dot3(right, two)
        at = slice(t * size, (t + 1) * size)
        out[:, at] = trailing[:, at] - keep * update


def call(kernel, scalars, arrays, shapes, flops):
    specs = [pl.BlockSpec(memory_space=pltpu.SMEM)] * len(scalars)
    specs += [pl.BlockSpec(memory_space=pltpu.VMEM)] * len(arrays)
    return pl.pallas_call(
        kernel,
        in_specs=specs,
        out_specs=[pl.BlockSpec(memory_space=pltpu.VMEM)] * len(shapes),
        out_shape=[jax.ShapeDtypeStruct(shape, jnp.float32) for shape in shapes],
        compiler_params=pltpu.CompilerParams(vmem_limit_bytes=16 << 20),
        cost_estimate=pl.CostEstimate(flops=flops, bytes_accessed=1 << 20, transcendentals=0),
    )(*scalars, *arrays)


def copies(x, count):
    return jnp.broadcast_to(x[None], (count,) + x.shape)


def pick(x, at, axis):
    return lax.dynamic_index_in_dim(x, at, axis, keepdims=False)


def local(panel, trailing, pattern, target_rows):
    _, size, width = panel.shape
    half = width // 2
    plane = ("y", "core")
    nz, npl = lax.axis_size("z"), lax.axis_size(plane)
    row = (lax.axis_index("z") * npl + lax.axis_index(plane)).astype(jnp.int32)[None]
    count = target_rows.shape[0]
    own = panel[0]
    nx = lax.axis_size("x")
    coarse, fine, lanes = size // npl, size // (npl * nx), width // 128
    assert coarse * lanes == 8 * nz and fine == 8 and lanes * 4 == nz
    pieces = lax.all_to_all(own.reshape(npl, coarse, width), plane, 0, 0)
    chosen = jnp.stack([pick(pieces, target_rows[t] % npl, 0) for t in range(count)])
    chosen = chosen.reshape(count, coarse // 8, 8, lanes, 128).transpose(1, 3, 0, 2, 4)
    share = lax.dynamic_slice_in_dim(pieces[:2], lax.axis_index("x") * fine, fine, 1)
    share = share.reshape(2, 2, 4, lanes, 128).transpose(0, 3, 1, 2, 4)
    part = jnp.concatenate(
        [chosen.reshape(nz, 2 * count, 4, 128), share.reshape(nz, 1, 4, 128)], axis=1
    )
    got = lax.all_to_all(part, "z", 0, 0)
    part = [
        lax.dynamic_slice(got, (target_rows[t] // npl, 2 * t, 0, 0), (1, 2, 4, 128))[0]
        for t in range(count)
    ]
    part = jnp.concatenate(part + [got[0, 2 * count :]])
    part = lax.all_to_all(copies(part, nz), "z", 0, 0)
    held = part[:, : 2 * count].reshape(coarse // 8, lanes, count, 8, 128)
    held = held.transpose(2, 0, 3, 1, 4).reshape(count, coarse, width)
    share = part[:, 2 * count].reshape(2, lanes, 8, 128)
    share = jnp.concatenate([share[0, : lanes // 2], share[1]])
    blocks = lax.all_to_all(copies(share, LINES * nx), ("y", "x"), 0, 0)
    blocks = lax.all_gather(blocks, "core", axis=0)
    blocks = blocks.reshape((CORES, LINES, nx) + share.shape)
    targets = lax.all_to_all(copies(held, npl), plane, 0, 0)
    (solver,) = call(pivot_kernel, (), (blocks,), ((3, size, half),), 1 << 34)
    mine, schur = call(
        update_kernel,
        (row, pattern, target_rows),
        (targets, solver, own, trailing[0]),
        ((size, width), (size, trailing.shape[2])),
        1 << 30,
    )
    return mine[None], schur[None]


def solution(mesh):
    blk, col = mesh.devices.shape
    inner = mesh.devices.reshape(blk // (LINES * CORES), LINES, CORES, col)
    inner = Mesh(inner, ("z", "y", "core", "x"))
    rows = ("z", "y", "core")
    in_specs = (P(None, rows, None), P(None, rows, "x"), P(), P("x"))
    out_specs = (P(None, rows, None), P(None, rows, "x"))
    return jax.shard_map(local, mesh=inner, in_specs=in_specs, out_specs=out_specs, check_vma=False)
```

```python
import jax
import jax.numpy as jnp
from jax import lax
from jax.experimental import pallas as pl
from jax.experimental.pallas import tpu as pltpu
from jax.sharding import Mesh, PartitionSpec as P

LINES, CORES = 4, 2
PANEL, STEP = 32, 16
OUTER = (((0,), (0,)), ((), ()))
ROWS = (((1,), (1,)), ((), ()))


def split(x):
    high = x.astype(jnp.bfloat16)
    rest = x - high.astype(jnp.float32)
    mid = rest.astype(jnp.bfloat16)
    low = (rest - mid.astype(jnp.float32)).astype(jnp.bfloat16)
    return high, mid, low


def outer(left, right):
    a, b, c = split(left)
    h, m, l = split(right)
    return lax.dot_general(
        jnp.concatenate([a, a, b, a, b, c], axis=0),
        jnp.concatenate([h, m, h, l, m, h], axis=0),
        OUTER,
        preferred_element_type=jnp.float32,
    )


def lane_block(x, lo, count):
    lane = lax.broadcasted_iota(jnp.int32, x.shape, 1)
    return (lane >= lo) & (lane < lo + count)


def inverse_factor(matrix):
    n = matrix.shape[0]
    groups, tiles = PANEL // 8, n // 128
    sub = lax.broadcasted_iota(jnp.int32, (8, 128), 0)
    lane = lax.broadcasted_iota(jnp.int32, (8, 128), 1)
    rest = matrix
    done = []
    for j in range(n // PANEL):
        lo = PANEL * j
        rows, rest = rest[:PANEL], rest[PANEL:]
        tile, off = lo // 128, lo % 128
        u = [
            [rows[8 * g : 8 * g + 8, 128 * c : 128 * c + 128] for c in range(tiles)]
            for g in range(groups)
        ]
        for g in range(groups):
            eye = (lane - off == sub + 8 * g).astype(jnp.float32)
            u[g][tile] = jnp.where(lane_block(eye, off, PANEL), eye, u[g][tile])
        scale = [jnp.zeros((8, 128), jnp.float32)] * groups
        block = [rows[8 * g : 8 * g + 8, 128 * tile : 128 * tile + 128] for g in range(groups)]
        for start in range(0, PANEL, STEP):
            stop = start + STEP
            cols = {
                k: {
                    g: jnp.broadcast_to(block[g][:, off + k : off + k + 1], (8, 128))
                    for g in range(k // 8, groups)
                }
                for k in range(start, stop)
            }

            def spread(i, k, cols=cols):
                return jnp.broadcast_to(cols[k][i // 8][i % 8 : i % 8 + 1], (8, 128))

            d = spread(start, start)
            b1 = spread(start + 1, start)
            for k in range(start, stop):
                at, s = k // 8, k % 8
                col = cols[k]
                r = pl.reciprocal(d, approx=True)
                scale[at] = jnp.where(sub == s, lax.rsqrt(d), scale[at])
                low = {g: jnp.where(sub > s, x, 0.0) if g == at else x for g, x in col.items()}
                ratio = {g: x * r for g, x in low.items()}
                if k + 1 < stop:
                    b = b1
                    d = spread(k + 1, k + 1) - (b * b) * r
                    if k + 2 < stop:
                        b1 = spread(k + 2, k + 1) - (spread(k + 2, k) * b) * r
                    for g in cols[k + 1]:
                        cols[k + 1][g] = cols[k + 1][g] - (low[g] * b) * r
                for i in range(k + 2, stop):
                    b = spread(i, k)
                    for g in cols[i]:
                        cols[i][g] = cols[i][g] - ratio[g] * b
                if stop < PANEL:
                    b = jnp.broadcast_to(block[at][s : s + 1], (8, 128))
                    for g in range(at if s < 7 else at + 1, groups):
                        block[g] = block[g] - ratio[g] * b
                for c in range(tiles):
                    b = jnp.broadcast_to(u[at][c][s : s + 1], (8, 128))
                    for g in range(at if s < 7 else at + 1, groups):
                        u[g][c] = u[g][c] - ratio[g] * b
        u = jnp.concatenate(
            [
                jnp.concatenate([x * scale[g] for x in u[g]], axis=1)
                for g in range(groups)
            ],
            axis=0,
        )
        done.append(u)
        left = rest.shape[0]
        if left:
            update = outer(u[:, 128 * ((lo + PANEL) // 128) :], u)
            update = update[update.shape[0] - left :]
            rest = jnp.where(lane_block(rest, lo, PANEL), 0.0, rest) - update
    full = jnp.concatenate(done, axis=0)
    row = lax.broadcasted_iota(jnp.int32, full.shape, 0)
    column = lax.broadcasted_iota(jnp.int32, full.shape, 1)
    return jnp.where(row >= column, full, 0.0)


def dot6(left, right):
    a, b, c = left
    h, m, l = right
    return lax.dot_general(
        jnp.concatenate([a, a, b, a, b, c], axis=1),
        jnp.concatenate([h, m, h, l, m, h], axis=1),
        ROWS,
        preferred_element_type=jnp.float32,
    )


def dot3(left, right):
    a, b, _ = left
    h, m, _ = right
    return lax.dot_general(
        jnp.concatenate([a, a, b], axis=1),
        jnp.concatenate([h, m, h], axis=1),
        ROWS,
        preferred_element_type=jnp.float32,
    )


def flag(pattern, part, row):
    return pattern[part, row].astype(jnp.float32)


def pivot_kernel(blocks, solver):
    size, half = solver.shape[1:]
    cores, lines, planes = blocks.shape[:3]

    def gather(k):
        rows = [
            [blocks[c, y, x, 2 * k + i] for i in range(2)]
            for y in range(lines)
            for c in range(cores)
            for x in range(planes)
        ]
        return jnp.concatenate([jnp.concatenate(tiles, axis=1) for tiles in rows])

    w00 = inverse_factor(gather(0))
    solver[0] = w00
    l10 = dot6(split(gather(1)), split(w00))
    solver[1] = l10
    l10 = split(l10)
    solver[2] = inverse_factor(gather(2) - dot6(l10, l10))


def update_kernel(row_ref, pattern, rows, targets, solver, own, trailing, mine, out):
    size, width = own.shape
    half = width // 2
    row = row_ref[0]
    w00, l10, w11 = split(solver[0]), split(solver[1]), split(solver[2])
    one = dot6(split(own[:, :half] * flag(pattern, 0, row)), w00)
    inner = own[:, half:] * flag(pattern, 1, row) - dot6(split(one), l10)
    two = dot6(split(inner), w11)
    shape = (size, half)
    upper = lax.broadcasted_iota(jnp.int32, shape, 0) < lax.broadcasted_iota(jnp.int32, shape, 1)
    one = jnp.where(upper & (row == 0), 0.0, one)
    two = jnp.where((upper & (row == 1)) | (row == 0), 0.0, two)
    mine[:, :half] = one
    mine[:, half:] = two
    left, right = split(one), split(two)
    keep = (row >= 2).astype(jnp.float32)
    for t in range(targets.shape[1]):
        block = targets[:, t].reshape(size, width)
        one = split(dot3(split(block[:, :half] * flag(pattern, 0, rows[t])), w00))
        inner = block[:, half:] * flag(pattern, 1, rows[t]) - dot3(one, l10)
        two = split(dot3(split(inner), w11))
        update = dot3(left, one) + dot3(right, two)
        at = slice(t * size, (t + 1) * size)
        out[:, at] = trailing[:, at] - keep * update


def call(kernel, scalars, arrays, shapes, flops):
    specs = [pl.BlockSpec(memory_space=pltpu.SMEM)] * len(scalars)
    specs += [pl.BlockSpec(memory_space=pltpu.VMEM)] * len(arrays)
    return pl.pallas_call(
        kernel,
        in_specs=specs,
        out_specs=[pl.BlockSpec(memory_space=pltpu.VMEM)] * len(shapes),
        out_shape=[jax.ShapeDtypeStruct(shape, jnp.float32) for shape in shapes],
        compiler_params=pltpu.CompilerParams(vmem_limit_bytes=16 << 20),
        cost_estimate=pl.CostEstimate(flops=flops, bytes_accessed=1 << 20, transcendentals=0),
    )(*scalars, *arrays)


def copies(x, count):
    return jnp.broadcast_to(x[None], (count,) + x.shape)


def pick(x, at, axis):
    return lax.dynamic_index_in_dim(x, at, axis, keepdims=False)


def local(panel, trailing, pattern, target_rows):
    _, size, width = panel.shape
    half = width // 2
    plane = ("y", "core")
    nz, npl = lax.axis_size("z"), lax.axis_size(plane)
    row = (lax.axis_index("z") * npl + lax.axis_index(plane)).astype(jnp.int32)[None]
    count = target_rows.shape[0]
    own = panel[0]
    nx = lax.axis_size("x")
    coarse, fine, lanes = size // npl, size // (npl * nx), width // 128
    assert coarse * lanes == 8 * nz and fine == 8 and lanes * 4 == nz
    pieces = lax.all_to_all(own.reshape(npl, coarse, width), plane, 0, 0)
    chosen = jnp.stack([pick(pieces, target_rows[t] % npl, 0) for t in range(count)])
    chosen = chosen.reshape(count, coarse // 8, 8, lanes, 128).transpose(1, 3, 0, 2, 4)
    share = lax.dynamic_slice_in_dim(pieces[:2], lax.axis_index("x") * fine, fine, 1)
    share = share.reshape(2, 2, 4, lanes, 128).transpose(0, 3, 1, 2, 4)
    part = jnp.concatenate(
        [chosen.reshape(nz, 2 * count, 4, 128), share.reshape(nz, 1, 4, 128)], axis=1
    )
    got = lax.all_to_all(part, "z", 0, 0)
    part = [
        lax.dynamic_slice(got, (target_rows[t] // npl, 2 * t, 0, 0), (1, 2, 4, 128))[0]
        for t in range(count)
    ]
    part = jnp.concatenate(part + [got[0, 2 * count :]])
    part = lax.all_to_all(copies(part, nz), "z", 0, 0)
    held = part[:, : 2 * count].reshape(coarse // 8, lanes, count, 8, 128)
    held = held.transpose(2, 0, 3, 1, 4).reshape(count, coarse, width)
    share = part[:, 2 * count].reshape(2, lanes, 8, 128)
    share = jnp.concatenate([share[0, : lanes // 2], share[1]])
    blocks = lax.all_to_all(copies(share, LINES * nx), ("y", "x"), 0, 0)
    blocks = lax.all_gather(blocks, "core", axis=0)
    blocks = blocks.reshape((CORES, LINES, nx) + share.shape)
    targets = lax.all_to_all(copies(held, npl), plane, 0, 0)
    (solver,) = call(pivot_kernel, (), (blocks,), ((3, size, half),), 1 << 34)
    mine, schur = call(
        update_kernel,
        (row, pattern, target_rows),
        (targets, solver, own, trailing[0]),
        ((size, width), (size, trailing.shape[2])),
        1 << 30,
    )
    return mine[None], schur[None]


def solution(mesh):
    blk, col = mesh.devices.shape
    inner = mesh.devices.reshape(blk // (LINES * CORES), LINES, CORES, col)
    inner = Mesh(inner, ("z", "y", "core", "x"))
    rows = ("z", "y", "core")
    in_specs = (P(None, rows, None), P(None, rows, "x"), P(), P("x"))
    out_specs = (P(None, rows, None), P(None, rows, "x"))
    return jax.shard_map(local, mesh=inner, in_specs=in_specs, out_specs=out_specs, check_vma=False)
```

```python
import jax
import jax.numpy as jnp
from jax import lax
from jax.experimental import pallas as pl
from jax.experimental.pallas import tpu as pltpu
from jax.sharding import Mesh, PartitionSpec as P

LINES, CORES = 4, 2
PANEL, STEP = 32, 16
OUTER = (((0,), (0,)), ((), ()))
ROWS = (((1,), (1,)), ((), ()))


def split(x):
    high = x.astype(jnp.bfloat16)
    rest = x - high.astype(jnp.float32)
    mid = rest.astype(jnp.bfloat16)
    low = (rest - mid.astype(jnp.float32)).astype(jnp.bfloat16)
    return high, mid, low


def outer(left, right):
    a, b, c = split(left)
    h, m, l = split(right)
    return lax.dot_general(
        jnp.concatenate([a, a, b, a, b, c], axis=0),
        jnp.concatenate([h, m, h, l, m, h], axis=0),
        OUTER,
        preferred_element_type=jnp.float32,
    )


def lane_block(x, lo, count):
    lane = lax.broadcasted_iota(jnp.int32, x.shape, 1)
    return (lane >= lo) & (lane < lo + count)


def inverse_factor(matrix):
    n = matrix.shape[0]
    groups, tiles = PANEL // 8, n // 128
    sub = lax.broadcasted_iota(jnp.int32, (8, 128), 0)
    lane = lax.broadcasted_iota(jnp.int32, (8, 128), 1)
    rest = matrix
    done = []
    for j in range(n // PANEL):
        lo = PANEL * j
        rows, rest = rest[:PANEL], rest[PANEL:]
        tile, off = lo // 128, lo % 128
        u = [
            [rows[8 * g : 8 * g + 8, 128 * c : 128 * c + 128] for c in range(tiles)]
            for g in range(groups)
        ]
        for g in range(groups):
            eye = (lane - off == sub + 8 * g).astype(jnp.float32)
            u[g][tile] = jnp.where(lane_block(eye, off, PANEL), eye, u[g][tile])
        scale = [jnp.zeros((8, 128), jnp.float32)] * groups
        block = [rows[8 * g : 8 * g + 8, 128 * tile : 128 * tile + 128] for g in range(groups)]
        for start in range(0, PANEL, STEP):
            stop = start + STEP
            cols = {
                k: {
                    g: jnp.broadcast_to(block[g][:, off + k : off + k + 1], (8, 128))
                    for g in range(k // 8, groups)
                }
                for k in range(start, stop)
            }

            def spread(i, k, cols=cols):
                return jnp.broadcast_to(cols[k][i // 8][i % 8 : i % 8 + 1], (8, 128))

            d = spread(start, start)
            b1 = spread(start + 1, start)
            for k in range(start, stop):
                at, s = k // 8, k % 8
                col = cols[k]
                r = pl.reciprocal(d, approx=True)
                scale[at] = jnp.where(sub == s, lax.rsqrt(d), scale[at])
                low = {g: jnp.where(sub > s, x, 0.0) if g == at else x for g, x in col.items()}
                ratio = {g: x * r for g, x in low.items()}
                if k + 1 < stop:
                    b = b1
                    d = spread(k + 1, k + 1) - (b * b) * r
                    if k + 2 < stop:
                        b1 = spread(k + 2, k + 1) - (spread(k + 2, k) * b) * r
                    for g in cols[k + 1]:
                        cols[k + 1][g] = cols[k + 1][g] - (low[g] * b) * r
                for i in range(k + 2, stop):
                    b = spread(i, k)
                    for g in cols[i]:
                        cols[i][g] = cols[i][g] - ratio[g] * b
                if stop < PANEL:
                    b = jnp.broadcast_to(block[at][s : s + 1], (8, 128))
                    for g in range(at if s < 7 else at + 1, groups):
                        block[g] = block[g] - ratio[g] * b
                for c in range(tiles):
                    b = jnp.broadcast_to(u[at][c][s : s + 1], (8, 128))
                    for g in range(at if s < 7 else at + 1, groups):
                        u[g][c] = u[g][c] - ratio[g] * b
        u = jnp.concatenate(
            [
                jnp.concatenate([x * scale[g] for x in u[g]], axis=1)
                for g in range(groups)
            ],
            axis=0,
        )
        done.append(u)
        left = rest.shape[0]
        if left:
            update = outer(u[:, 128 * ((lo + PANEL) // 128) :], u)
            update = update[update.shape[0] - left :]
            rest = jnp.where(lane_block(rest, lo, PANEL), 0.0, rest) - update
    full = jnp.concatenate(done, axis=0)
    row = lax.broadcasted_iota(jnp.int32, full.shape, 0)
    column = lax.broadcasted_iota(jnp.int32, full.shape, 1)
    return jnp.where(row >= column, full, 0.0)


def dot6(left, right):
    a, b, c = left
    h, m, l = right
    return lax.dot_general(
        jnp.concatenate([a, a, b, a, b, c], axis=1),
        jnp.concatenate([h, m, h, l, m, h], axis=1),
        ROWS,
        preferred_element_type=jnp.float32,
    )


def dot3(left, right):
    a, b, _ = left
    h, m, _ = right
    return lax.dot_general(
        jnp.concatenate([a, a, b], axis=1),
        jnp.concatenate([h, m, h], axis=1),
        ROWS,
        preferred_element_type=jnp.float32,
    )


def flag(pattern, part, row):
    return pattern[part, row].astype(jnp.float32)


def pivot_kernel(blocks, solver):
    size, half = solver.shape[1:]
    cores, lines, planes = blocks.shape[:3]

    def gather(k):
        rows = [
            [blocks[c, y, x, 2 * k + i] for i in range(2)]
            for y in range(lines)
            for c in range(cores)
            for x in range(planes)
        ]
        return jnp.concatenate([jnp.concatenate(tiles, axis=1) for tiles in rows])

    w00 = inverse_factor(gather(0))
    solver[0] = w00
    l10 = dot6(split(gather(1)), split(w00))
    solver[1] = l10
    l10 = split(l10)
    solver[2] = inverse_factor(gather(2) - dot6(l10, l10))


def update_kernel(
    row_ref, rows, pattern_ref, targets, solver, own, trailing, mine, out, pattern, done
):
    size, width = own.shape
    half = width // 2
    row = row_ref[0]
    fetch = pltpu.make_async_copy(pattern_ref, pattern, done)
    fetch.start()
    w00, l10, w11 = split(solver[0]), split(solver[1]), split(solver[2])
    one = dot3(split(own[:, :half]), w00)
    fetch.wait()
    one = jnp.where(pattern[0, row] != 0, one, 0.0)
    inner = own[:, half:] * flag(pattern, 1, row) - dot3(split(one), l10)
    two = dot3(split(inner), w11)
    shape = (size, half)
    upper = lax.broadcasted_iota(jnp.int32, shape, 0) < lax.broadcasted_iota(jnp.int32, shape, 1)
    one = jnp.where(upper & (row == 0), 0.0, one)
    two = jnp.where((upper & (row == 1)) | (row == 0), 0.0, two)
    mine[:, :half] = one
    mine[:, half:] = two
    left, right = split(one), split(two)
    keep = (row >= 2).astype(jnp.float32)
    for t in range(targets.shape[1]):
        block = targets[:, t].reshape(size, width)
        one = split(dot3(split(block[:, :half] * flag(pattern, 0, rows[t])), w00))
        inner = block[:, half:] * flag(pattern, 1, rows[t]) - dot3(one, l10)
        two = split(dot3(split(inner), w11))
        update = dot3(left, one) + dot3(right, two)
        at = slice(t * size, (t + 1) * size)
        out[:, at] = trailing[:, at] - keep * update


def call(kernel, scalars, arrays, shapes, flops, raw=(), scratch=()):
    specs = [pl.BlockSpec(memory_space=pltpu.SMEM)] * len(scalars)
    specs += [pl.BlockSpec(memory_space=pl.ANY)] * len(raw)
    specs += [pl.BlockSpec(memory_space=pltpu.VMEM)] * len(arrays)
    return pl.pallas_call(
        kernel,
        in_specs=specs,
        out_specs=[pl.BlockSpec(memory_space=pltpu.VMEM)] * len(shapes),
        out_shape=[jax.ShapeDtypeStruct(shape, jnp.float32) for shape in shapes],
        scratch_shapes=scratch,
        compiler_params=pltpu.CompilerParams(vmem_limit_bytes=16 << 20),
        cost_estimate=pl.CostEstimate(flops=flops, bytes_accessed=1 << 20, transcendentals=0),
    )(*scalars, *raw, *arrays)


def copies(x, count):
    return jnp.broadcast_to(x[None], (count,) + x.shape)


def pick(x, at, axis):
    return lax.dynamic_index_in_dim(x, at, axis, keepdims=False)


def local(panel, trailing, pattern, target_rows):
    _, size, width = panel.shape
    half = width // 2
    plane = ("y", "core")
    nz, npl = lax.axis_size("z"), lax.axis_size(plane)
    row = (lax.axis_index("z") * npl + lax.axis_index(plane)).astype(jnp.int32)[None]
    count = target_rows.shape[0]
    own = panel[0]
    nx = lax.axis_size("x")
    coarse, fine, lanes = size // npl, size // (npl * nx), width // 128
    assert coarse * lanes == 8 * nz and fine == 8 and lanes * 4 == nz
    pieces = lax.all_to_all(own.reshape(npl, coarse, width), plane, 0, 0)
    chosen = jnp.stack([pick(pieces, target_rows[t] % npl, 0) for t in range(count)])
    chosen = chosen.reshape(count, coarse // 8, 8, lanes, 128).transpose(1, 3, 0, 2, 4)
    share = lax.dynamic_slice_in_dim(pieces[:2], lax.axis_index("x") * fine, fine, 1)
    share = share.reshape(2, 2, 4, lanes, 128).transpose(0, 3, 1, 2, 4)
    part = jnp.concatenate(
        [chosen.reshape(nz, 2 * count, 4, 128), share.reshape(nz, 1, 4, 128)], axis=1
    )
    got = lax.all_to_all(part, "z", 0, 0)
    part = [
        lax.dynamic_slice(got, (target_rows[t] // npl, 2 * t, 0, 0), (1, 2, 4, 128))[0]
        for t in range(count)
    ]
    part = jnp.concatenate(part + [got[0, 2 * count :]])
    part = lax.all_to_all(copies(part, nz), "z", 0, 0)
    held = part[:, : 2 * count].reshape(coarse // 8, lanes, count, 8, 128)
    held = held.transpose(2, 0, 3, 1, 4).reshape(count, coarse, width)
    share = part[:, 2 * count].reshape(2, lanes, 8, 128)
    share = jnp.concatenate([share[0, : lanes // 2], share[1]])
    blocks = lax.all_to_all(copies(share, LINES * nx), ("y", "x"), 0, 0)
    blocks = lax.all_gather(blocks, "core", axis=0)
    blocks = blocks.reshape((CORES, LINES, nx) + share.shape)
    targets = lax.all_to_all(copies(held, npl), plane, 0, 0)
    (solver,) = call(pivot_kernel, (), (blocks,), ((3, size, half),), 1 << 34)
    mine, schur = call(
        update_kernel,
        (row, target_rows),
        (targets, solver, own, trailing[0]),
        ((size, width), (size, trailing.shape[2])),
        1 << 30,
        (pattern,),
        (pltpu.SMEM(pattern.shape, jnp.int32), pltpu.SemaphoreType.DMA),
    )
    return mine[None], schur[None]


def solution(mesh):
    blk, col = mesh.devices.shape
    inner = mesh.devices.reshape(blk // (LINES * CORES), LINES, CORES, col)
    inner = Mesh(inner, ("z", "y", "core", "x"))
    rows = ("z", "y", "core")
    in_specs = (P(None, rows, None), P(None, rows, "x"), P(), P("x"))
    out_specs = (P(None, rows, None), P(None, rows, "x"))
    return jax.shard_map(local, mesh=inner, in_specs=in_specs, out_specs=out_specs, check_vma=False)
```

```python
import jax
import jax.numpy as jnp
from jax import lax
from jax.experimental import pallas as pl
from jax.experimental.pallas import tpu as pltpu
from jax.sharding import Mesh, PartitionSpec as P

LINES, CORES = 4, 2
PANEL, STEP = 32, 16
OUTER = (((0,), (0,)), ((), ()))
ROWS = (((1,), (1,)), ((), ()))


def split(x):
    high = x.astype(jnp.bfloat16)
    rest = x - high.astype(jnp.float32)
    mid = rest.astype(jnp.bfloat16)
    low = (rest - mid.astype(jnp.float32)).astype(jnp.bfloat16)
    return high, mid, low


def outer(left, right):
    a, b, c = split(left)
    h, m, l = split(right)
    return lax.dot_general(
        jnp.concatenate([a, a, b, a, b, c], axis=0),
        jnp.concatenate([h, m, h, l, m, h], axis=0),
        OUTER,
        preferred_element_type=jnp.float32,
    )


def lane_block(x, lo, count):
    lane = lax.broadcasted_iota(jnp.int32, x.shape, 1)
    return (lane >= lo) & (lane < lo + count)


def inverse_factor(matrix):
    n = matrix.shape[0]
    groups, tiles = PANEL // 8, n // 128
    sub = lax.broadcasted_iota(jnp.int32, (8, 128), 0)
    lane = lax.broadcasted_iota(jnp.int32, (8, 128), 1)
    rest = matrix
    done = []
    for j in range(n // PANEL):
        lo = PANEL * j
        rows, rest = rest[:PANEL], rest[PANEL:]
        tile, off = lo // 128, lo % 128
        u = [
            [rows[8 * g : 8 * g + 8, 128 * c : 128 * c + 128] for c in range(tiles)]
            for g in range(groups)
        ]
        for g in range(groups):
            eye = (lane - off == sub + 8 * g).astype(jnp.float32)
            u[g][tile] = jnp.where(lane_block(eye, off, PANEL), eye, u[g][tile])
        scale = [jnp.zeros((8, 128), jnp.float32)] * groups
        block = [rows[8 * g : 8 * g + 8, 128 * tile : 128 * tile + 128] for g in range(groups)]
        for start in range(0, PANEL, STEP):
            stop = start + STEP
            cols = {
                k: {
                    g: jnp.broadcast_to(block[g][:, off + k : off + k + 1], (8, 128))
                    for g in range(k // 8, groups)
                }
                for k in range(start, stop)
            }

            def spread(i, k, cols=cols):
                return jnp.broadcast_to(cols[k][i // 8][i % 8 : i % 8 + 1], (8, 128))

            d = spread(start, start)
            b1 = spread(start + 1, start)
            for k in range(start, stop):
                at, s = k // 8, k % 8
                col = cols[k]
                r = pl.reciprocal(d, approx=True)
                scale[at] = jnp.where(sub == s, lax.rsqrt(d), scale[at])
                low = {g: jnp.where(sub > s, x, 0.0) if g == at else x for g, x in col.items()}
                ratio = {g: x * r for g, x in low.items()}
                if k + 1 < stop:
                    b = b1
                    d = spread(k + 1, k + 1) - (b * b) * r
                    if k + 2 < stop:
                        b1 = spread(k + 2, k + 1) - (spread(k + 2, k) * b) * r
                    for g in cols[k + 1]:
                        cols[k + 1][g] = cols[k + 1][g] - (low[g] * b) * r
                for i in range(k + 2, stop):
                    b = spread(i, k)
                    for g in cols[i]:
                        cols[i][g] = cols[i][g] - ratio[g] * b
                if stop < PANEL:
                    b = jnp.broadcast_to(block[at][s : s + 1], (8, 128))
                    for g in range(at if s < 7 else at + 1, groups):
                        block[g] = block[g] - ratio[g] * b
                for c in range(tiles):
                    b = jnp.broadcast_to(u[at][c][s : s + 1], (8, 128))
                    for g in range(at if s < 7 else at + 1, groups):
                        u[g][c] = u[g][c] - ratio[g] * b
        u = jnp.concatenate(
            [
                jnp.concatenate([x * scale[g] for x in u[g]], axis=1)
                for g in range(groups)
            ],
            axis=0,
        )
        done.append(u)
        left = rest.shape[0]
        if left:
            update = outer(u[:, 128 * ((lo + PANEL) // 128) :], u)
            update = update[update.shape[0] - left :]
            rest = jnp.where(lane_block(rest, lo, PANEL), 0.0, rest) - update
    full = jnp.concatenate(done, axis=0)
    row = lax.broadcasted_iota(jnp.int32, full.shape, 0)
    column = lax.broadcasted_iota(jnp.int32, full.shape, 1)
    return jnp.where(row >= column, full, 0.0)


def dot6(left, right):
    a, b, c = left
    h, m, l = right
    return lax.dot_general(
        jnp.concatenate([a, a, b, a, b, c], axis=1),
        jnp.concatenate([h, m, h, l, m, h], axis=1),
        ROWS,
        preferred_element_type=jnp.float32,
    )


def dot3(left, right):
    a, b, _ = left
    h, m, _ = right
    return lax.dot_general(
        jnp.concatenate([a, a, b], axis=1),
        jnp.concatenate([h, m, h], axis=1),
        ROWS,
        preferred_element_type=jnp.float32,
    )


def flag(pattern, part, row):
    return pattern[part, row].astype(jnp.float32)


def pivot_kernel(blocks, solver):
    size, half = solver.shape[1:]
    cores, lines, planes = blocks.shape[:3]

    def gather(k):
        rows = [
            [blocks[c, y, x, 2 * k + i] for i in range(2)]
            for y in range(lines)
            for c in range(cores)
            for x in range(planes)
        ]
        return jnp.concatenate([jnp.concatenate(tiles, axis=1) for tiles in rows])

    w00 = inverse_factor(gather(0))
    solver[0] = w00
    l10 = dot6(split(gather(1)), split(w00))
    solver[1] = l10
    l10 = split(l10)
    solver[2] = inverse_factor(gather(2) - dot6(l10, l10))


def update_kernel(row_ref, pattern, rows, targets, solver, own, trailing, mine, out):
    size, width = own.shape
    half = width // 2
    row = row_ref[0]
    w00, l10, w11 = split(solver[0]), split(solver[1]), split(solver[2])
    one = dot3(split(own[:, :half] * flag(pattern, 0, row)), w00)
    inner = own[:, half:] * flag(pattern, 1, row) - dot3(split(one), l10)
    two = dot3(split(inner), w11)
    shape = (size, half)
    upper = lax.broadcasted_iota(jnp.int32, shape, 0) < lax.broadcasted_iota(jnp.int32, shape, 1)
    one = jnp.where(upper & (row == 0), 0.0, one)
    two = jnp.where((upper & (row == 1)) | (row == 0), 0.0, two)
    mine[:, :half] = one
    mine[:, half:] = two
    left, right = split(one), split(two)
    keep = (row >= 2).astype(jnp.float32)
    for t in range(targets.shape[1]):
        block = targets[:, t].reshape(size, width)
        one = split(dot3(split(block[:, :half] * flag(pattern, 0, rows[t])), w00))
        inner = block[:, half:] * flag(pattern, 1, rows[t]) - dot3(one, l10)
        two = split(dot3(split(inner), w11))
        update = dot3(left, one) + dot3(right, two)
        at = slice(t * size, (t + 1) * size)
        out[:, at] = trailing[:, at] - keep * update


def call(kernel, scalars, arrays, shapes, flops):
    specs = [pl.BlockSpec(memory_space=pltpu.SMEM)] * len(scalars)
    specs += [pl.BlockSpec(memory_space=pltpu.VMEM)] * len(arrays)
    return pl.pallas_call(
        kernel,
        in_specs=specs,
        out_specs=[pl.BlockSpec(memory_space=pltpu.VMEM)] * len(shapes),
        out_shape=[jax.ShapeDtypeStruct(shape, jnp.float32) for shape in shapes],
        compiler_params=pltpu.CompilerParams(vmem_limit_bytes=16 << 20),
        cost_estimate=pl.CostEstimate(flops=flops, bytes_accessed=1 << 20, transcendentals=0),
    )(*scalars, *arrays)


def copies(x, count):
    return jnp.broadcast_to(x[None], (count,) + x.shape)


def pick(x, at, axis):
    return lax.dynamic_index_in_dim(x, at, axis, keepdims=False)


def local(panel, trailing, pattern, target_rows):
    _, size, width = panel.shape
    half = width // 2
    plane = ("y", "core")
    nz, npl = lax.axis_size("z"), lax.axis_size(plane)
    row = (lax.axis_index("z") * npl + lax.axis_index(plane)).astype(jnp.int32)[None]
    count = target_rows.shape[0]
    own = panel[0]
    nx = lax.axis_size("x")
    coarse, fine, lanes = size // npl, size // (npl * nx), width // 128
    assert coarse * lanes == 8 * nz and fine == 8 and lanes * 4 == nz
    pieces = lax.all_to_all(own.reshape(npl, coarse, width), plane, 0, 0)
    chosen = jnp.stack([pick(pieces, target_rows[t] % npl, 0) for t in range(count)])
    chosen = chosen.reshape(count, coarse // 8, 8, lanes, 128).transpose(1, 3, 0, 2, 4)
    share = lax.dynamic_slice_in_dim(pieces[:2], lax.axis_index("x") * fine, fine, 1)
    share = share.reshape(2, 2, 4, lanes, 128).transpose(0, 3, 1, 2, 4)
    part = jnp.concatenate(
        [chosen.reshape(nz, 2 * count, 4, 128), share.reshape(nz, 1, 4, 128)], axis=1
    )
    got = lax.all_to_all(part, "z", 0, 0)
    part = [
        lax.dynamic_slice(got, (target_rows[t] // npl, 2 * t, 0, 0), (1, 2, 4, 128))[0]
        for t in range(count)
    ]
    part = jnp.concatenate(part + [got[0, 2 * count :]])
    part = lax.all_to_all(copies(part, nz), "z", 0, 0)
    held = part[:, : 2 * count].reshape(coarse // 8, lanes, count, 8, 128)
    held = held.transpose(2, 0, 3, 1, 4).reshape(count, coarse, width)
    share = part[:, 2 * count].reshape(2, lanes, 8, 128)
    share = jnp.concatenate([share[0, : lanes // 2], share[1]])
    blocks = lax.all_to_all(copies(share, LINES * nx), ("y", "x"), 0, 0)
    blocks = lax.all_gather(blocks, "core", axis=0)
    blocks = blocks.reshape((CORES, LINES, nx) + share.shape)
    targets = lax.all_to_all(copies(held, npl), plane, 0, 0)
    (solver,) = call(pivot_kernel, (), (blocks,), ((3, size, half),), 1 << 34)
    mine, schur = call(
        update_kernel,
        (row, pattern, target_rows),
        (targets, solver, own, trailing[0]),
        ((size, width), (size, trailing.shape[2])),
        1 << 30,
    )
    return mine[None], schur[None]


def solution(mesh):
    blk, col = mesh.devices.shape
    inner = mesh.devices.reshape(blk // (LINES * CORES), LINES, CORES, col)
    inner = Mesh(inner, ("z", "y", "core", "x"))
    rows = ("z", "y", "core")
    in_specs = (P(None, rows, None), P(None, rows, "x"), P(), P("x"))
    out_specs = (P(None, rows, None), P(None, rows, "x"))
    return jax.shard_map(local, mesh=inner, in_specs=in_specs, out_specs=out_specs, check_vma=False)
```
